32 devices in a mesh: section: 2 (over y), dp: 8 (over z, core), tensor: 2 (over x).
Axes of the slice: x: 2, y: 2, z: 4, core: 2. Of those that a mesh axis runs over, the one named last changes fastest.
Arguments:
- section_inputs: bfloat16 [2, 128, 2560], P('section', 'dp', 'tensor'), may hold values from -40 to 40
- entering: bfloat16 [1, 128, 2560], P(None, 'dp', 'tensor'), may hold values from -40 to 40
- grad_outputs: bfloat16 [2, 128, 2560], P('section', 'dp', 'tensor'), may hold values from -6 to 6
- arriving: bfloat16 [1, 128, 2560], P(None, 'dp', 'tensor'), may hold values from -6 to 6
- live_rows: int32 [1], replicated, may hold values from 64 to 128
- stashed_inputs: bfloat16 [2, 2, 128, 2560], P('section', None, 'dp', 'tensor'), may hold values from -40 to 40
- norm_gain: bfloat16 [2, 2560], P('section', 'tensor'), may hold values from 0.25 to 1.75
- up_weight: bfloat16 [2, 2560, 14336], P('section', 'tensor', 'dp'), may hold values from -0.125 to 0.125
- down_weight: bfloat16 [2, 14336, 2560], P('section', 'dp', 'tensor'), may hold values from -0.046875 to 0.046875
- held_blocks: int32 [2, 2, 8, 6], P('section', 'tensor'), may hold values from 0 to 279, as said below
- held_count: int32 [2, 2, 8], P('section', 'tensor'), may hold values from 1 to 6, as said below
- held_owner: int32 [2, 2, 8, 6], P('section', 'tensor'), may hold values from 0 to 7, as said below
- first_moment: float32 [2, 2, 8, 6, 128, 128], P('section', 'tensor', 'dp'), may hold values from -4 to 4
- second_moment: float32 [2, 2, 8, 6, 128, 128], P('section', 'tensor', 'dp'), may hold values from 0.01 to 1
Outputs:
- section_outputs: bfloat16 [2, 2, 128, 2560], P('section', None, 'dp', 'tensor')
- input_grads: bfloat16 [2, 2, 128, 2560], P('section', None, 'dp', 'tensor')
- first_next: float32 [2, 2, 8, 6, 128, 128], P('section', 'tensor', 'dp')
- second_next: float32 [2, 2, 8, 6, 128, 128], P('section', 'tensor', 'dp')
- update_direction: float32 [2, 2, 8, 6, 128, 128], P('section', 'tensor', 'dp')
The draws below stay inside these ranges and needn't reach their ends.
Inputs may be any that keep to these rules, and one draw needn't show every extreme that they name: `held_blocks`: A number below 140 names a block of the device's up projection share, row-major over 10 x 14 blocks; the others, less 140, a block of its down projection share, row-major over 14 x 10 blocks. A device's first held_count entries are distinct; later entries are not used. `held_count`: some device of each section and tensor index lists 6 trainable blocks. `held_owner`: the owners of one device's trainable blocks are distinct and never the device itself. Each dp index owns at most 6 blocks of one section and tensor index, and some owns exactly 6.
All inputs are finite; a program needn't handle non-finite values.
Results may differ from the reference program's by a relative error of at most 0.015.
Values may be sent and summed in bfloat16 or wider, within the bound.
No kernel may reach another device: no remote copies, remote signals or barrier semaphores. Data moves between devices by JAX's collectives and lax.ppermute only.
A program may use at most 64 MiB of HBM per device.

```python
import math
import jax
import jax.numpy as jnp
from jax import lax

DW = 2560
FF = 14336
BLK = 128
TURNS = 2
ROWS = 128
HCAP = 6
N_SECTION = 2
N_DP = 8
N_TENSOR = 2


def spread_rows(key, leading):
    key_base, key_rows, key_cols = jax.random.split(key, 3)
    full_shape = leading + (ROWS, DW)
    samples = jnp.clip(jax.random.normal(key_base, full_shape, jnp.float32), -4.0, 4.0)
    row_scales = jnp.power(10.0, jax.random.uniform(key_rows, leading + (ROWS, 1), jnp.float32, -0.5, 0.5))
    col_scales = jnp.power(10.0, jax.random.uniform(key_cols, leading + (1, DW), jnp.float32, -0.5, 0.5))
    return (samples * row_scales * col_scales).astype(jnp.bfloat16)


def draw_section_inputs(key, part):
    return spread_rows(key, (N_SECTION,))


def draw_entering(key, part):
    return spread_rows(key, (TURNS - 1,))


def draw_stashed_inputs(key, part):
    return spread_rows(key, (N_SECTION, TURNS))


def ownership(key):
    capacity = HCAP
    light_top = max(2, capacity // 2)

    def column(column_key):
        key_order, key_light, key_turn = jax.random.split(column_key, 3)
        cyclic_order = jax.random.permutation(key_order, N_DP).astype(jnp.int32)
        position = jnp.argsort(cyclic_order).astype(jnp.int32)
        light_counts = jax.random.randint(key_light, (N_DP,), 1, light_top + 1)
        counts_by_position = jnp.where(jnp.arange(N_DP) < capacity, capacity, light_counts)
        counts = counts_by_position[position]
        rotation = jax.random.randint(key_turn, (N_DP,), 0, capacity)
        slot_ids = jnp.arange(capacity)
        offsets = (slot_ids[None, :] + rotation[:, None]) % capacity + 1
        owners = cyclic_order[(position[:, None] + offsets) % N_DP]
        return (counts.astype(jnp.int32), owners.astype(jnp.int32))
    key_list = jax.random.split(jax.random.fold_in(key, 11), N_SECTION * N_TENSOR)
    counts, owners = jax.vmap(column)(key_list)
    return (counts.reshape(N_SECTION, N_TENSOR, N_DP), owners.reshape(N_SECTION, N_TENSOR, N_DP, HCAP))


def draw_held_count(key, part):
    return ownership(key)[0]


def draw_held_owner(key, part):
    return ownership(key)[1]


def draw_held_blocks(key, part):
    block_total = 2 * (DW // (N_TENSOR * BLK)) * (FF // (N_DP * BLK))
    key_list = jax.random.split(jax.random.fold_in(key, 5), N_SECTION * N_TENSOR * N_DP)
    chosen_ids = jax.vmap(lambda one_key: jax.random.permutation(one_key, block_total)[:HCAP])(key_list)
    return chosen_ids.reshape(N_SECTION, N_TENSOR, N_DP, HCAP).astype(jnp.int32)


def block_scale(rng, shape, shards, smallest, high):
    loudness = 1.0
    for dim, parts in shards:
        heights = jax.random.uniform(jax.random.fold_in(jax.random.fold_in(rng, 6), dim), (parts,), jnp.float32, smallest / len(shards), high / len(shards))
        loudness = loudness * jnp.repeat(jnp.exp(heights), shape[dim] // parts).reshape((-1,) + (1,) * (len(shape) - 1 - dim))
    return loudness


def gaussian(key, dims, deviation, bound, pieces=(), kind=jnp.bfloat16):
    values = jax.random.normal(key, dims, jnp.float32) * deviation
    if len(pieces) > 0:
        values = block_scale(key, dims, pieces, -0.22, 0.18) * values
    return jnp.clip(values, min=-bound, max=bound).astype(kind)


def setup_inputs(seed: int = 0) -> dict:
    seeds = jax.random.split(jax.random.key(seed), 15)
    return {
        "section_inputs": draw_section_inputs(jax.random.fold_in(seeds[14], 71), 0),
        "entering": draw_entering(jax.random.fold_in(seeds[14], 71), 0),
        "grad_outputs": gaussian(seeds[2], (N_SECTION, ROWS, DW), 1.0, 6.0, ((0, 2), (1, 8), (2, 2))),
        "arriving": gaussian(seeds[3], (TURNS - 1, ROWS, DW), 1.0, 6.0, ((1, 8), (2, 2))),
        "live_rows": jax.random.randint(seeds[4], (TURNS - 1,), ROWS // 2, ROWS + 1).astype(jnp.int32),
        "stashed_inputs": draw_stashed_inputs(jax.random.fold_in(seeds[14], 71), 0),
        "norm_gain": jnp.clip(1.0 + 0.15 * jax.random.normal(seeds[6], (N_SECTION, DW), jnp.float32), 0.25, 1.75).astype(jnp.bfloat16),
        "up_weight": gaussian(seeds[7], (N_SECTION, DW, FF), DW ** -0.5, 0.125, ((0, 2), (1, 2), (2, 8))),
        "down_weight": gaussian(seeds[8], (N_SECTION, FF, DW), FF ** -0.5, 0.046875, ((0, 2), (1, 8), (2, 2))),
        "held_blocks": draw_held_blocks(jax.random.fold_in(seeds[14], 71), 0),
        "held_count": draw_held_count(jax.random.fold_in(seeds[14], 71), 0),
        "held_owner": draw_held_owner(jax.random.fold_in(seeds[14], 71), 0),
        "first_moment": gaussian(seeds[12], (N_SECTION, N_TENSOR, N_DP, HCAP, BLK, BLK), 1.0, 4.0, ((0, 2), (1, 2), (2, 8)), jnp.float32),
        "second_moment": jnp.clip(jnp.exp(math.log(1.0) - 4.6051702 * jax.random.uniform(seeds[13], (N_SECTION, N_TENSOR, N_DP, HCAP, BLK, BLK), jnp.float32) ** block_scale(seeds[13], (N_SECTION, N_TENSOR, N_DP, HCAP, BLK, BLK), ((0, 2), (1, 2), (2, 8)), -0.2, 0.2)), 0.01, 1.0),
    }


EPSILON = 1e-06

def normed_product(rows_in, gain_row, up_matrix):
    widened = rows_in.astype(jnp.float32)
    squares = lax.optimization_barrier(jnp.sum(widened * widened, axis=1))
    normed = (widened * gain_row.astype(jnp.float32)).astype(jnp.bfloat16)
    product = jnp.dot(normed, up_matrix, preferred_element_type=jnp.float32)
    row_scales = lax.rsqrt(squares / DW + EPSILON)
    return (normed, product, row_scales)

def layer_forward(rows_in, gain_row, up_matrix, down_matrix):
    normed, product, row_scales = normed_product(rows_in, gain_row, up_matrix)
    hidden = product * row_scales[:, None]
    activated = (hidden * jax.nn.sigmoid(hidden)).astype(jnp.bfloat16)
    mixed_rows = jnp.dot(activated, down_matrix, preferred_element_type=jnp.float32)
    return (rows_in.astype(jnp.float32) + mixed_rows).astype(jnp.bfloat16)

def block_gradients(normed, activated, scaled_grad, grads_in, held_list):
    channel_total = DW // BLK
    hidden_total = FF // BLK
    channel_blocks = DW // (N_TENSOR * BLK)
    hidden_blocks = FF // (N_DP * BLK)
    up_count = channel_blocks * hidden_blocks
    left_table = jnp.concatenate([normed.reshape(ROWS, channel_total, BLK), activated.reshape(ROWS, hidden_total, BLK)], axis=1)
    right_table = jnp.concatenate([scaled_grad.reshape(ROWS, hidden_total, BLK), grads_in.reshape(ROWS, channel_total, BLK)], axis=1)
    tensor_ids = jnp.arange(N_TENSOR, dtype=jnp.int32)[:, None, None]
    holder_ids = jnp.arange(N_DP, dtype=jnp.int32)[None, :, None]
    down_number = held_list - up_count
    is_up = held_list < up_count
    left_index = jnp.where(is_up, tensor_ids * channel_blocks + held_list // hidden_blocks, channel_total + holder_ids * hidden_blocks + down_number // channel_blocks)
    right_index = jnp.where(is_up, holder_ids * hidden_blocks + held_list % hidden_blocks, hidden_total + tensor_ids * channel_blocks + down_number % channel_blocks)
    left_pick = jnp.take(left_table, left_index.reshape(-1).astype(jnp.int32), axis=1).astype(jnp.float32)
    right_pick = jnp.take(right_table, right_index.reshape(-1).astype(jnp.int32), axis=1).astype(jnp.float32)
    block_grads = jnp.einsum('rkb,rkc->kbc', left_pick, right_pick)
    return block_grads.reshape(N_TENSOR, N_DP, HCAP, BLK, BLK)

def layer_backward(rows_in, grads_in, gain_row, up_matrix, down_matrix, held_list):
    normed, product, row_scales = normed_product(rows_in, gain_row, up_matrix)
    hidden = product * row_scales[:, None]
    sigmoid_part = jax.nn.sigmoid(hidden)
    activated = (hidden * sigmoid_part).astype(jnp.bfloat16)
    act_grad = jnp.dot(grads_in, down_matrix.T, preferred_element_type=jnp.float32)
    hidden_grad = act_grad * sigmoid_part * (1.0 + hidden * (1.0 - sigmoid_part))
    scaled_grad = (hidden_grad * row_scales[:, None]).astype(jnp.bfloat16)
    scale_grad = lax.optimization_barrier(jnp.sum(hidden_grad * product, axis=1))
    normed_grad = jnp.dot(scaled_grad, up_matrix.T, preferred_element_type=jnp.float32)
    widened = rows_in.astype(jnp.float32)
    input_grad = grads_in.astype(jnp.float32) + normed_grad * gain_row.astype(jnp.float32) - (scale_grad * row_scales ** 3)[:, None] * widened / DW
    block_grads = block_gradients(normed, activated, scaled_grad, grads_in, held_list)
    return (input_grad.astype(jnp.bfloat16), block_grads)

def route_blocks(block_grads, counts, owners):
    slot_ids = jnp.arange(HCAP, dtype=jnp.int32)
    dp_ids = jnp.arange(N_DP, dtype=jnp.int32)
    live_slots = slot_ids[None, None, :] < counts[:, :, None]
    chosen = (owners[:, :, None, :] == dp_ids[None, None, :, None]) & live_slots[:, :, None, :]
    is_sent = jnp.any(chosen, axis=3)
    slot_pick = lax.optimization_barrier(jnp.sum(jnp.where(chosen, slot_ids, 0), axis=3)).astype(jnp.int32)
    sent_grads = jnp.take_along_axis(block_grads, slot_pick[:, :, :, None, None], axis=2)
    sent_grads = jnp.where(is_sent[..., None, None], sent_grads, 0.0)
    sent_count = is_sent.astype(jnp.int32)
    ranks = jnp.cumsum(sent_count, axis=1) - sent_count
    matches = is_sent[:, :, :, None] & (ranks[:, :, :, None] == slot_ids)
    is_filled = jnp.any(matches, axis=1)
    source_ids = lax.optimization_barrier(jnp.sum(jnp.where(matches, dp_ids[None, :, None, None], 0), axis=1)).astype(jnp.int32)
    by_owner = jnp.swapaxes(sent_grads, 1, 2)
    owned_grads = jnp.take_along_axis(by_owner, source_ids[..., None, None], axis=2)
    owned_grads = jnp.where(is_filled[..., None, None], owned_grads, 0.0)
    return (owned_grads, is_filled)

def reference(section_inputs, entering, grad_outputs, arriving, live_rows, stashed_inputs, norm_gain, up_weight, down_weight, held_blocks, held_count, held_owner, first_moment, second_moment):
    forward_table = [[None] * TURNS for layer_index in range(N_SECTION)]
    for turn in range(TURNS):
        for layer_index in range(N_SECTION):
            if turn == 0:
                rows_in = section_inputs[layer_index]
            elif layer_index == 0:
                rows_in = entering[turn - 1]
            else:
                rows_in = forward_table[layer_index - 1][turn - 1]
            forward_table[layer_index][turn] = layer_forward(rows_in, norm_gain[layer_index], up_weight[layer_index], down_weight[layer_index])
    row_ids = jnp.arange(ROWS, dtype=jnp.int32)
    backward_table = [[None] * TURNS for layer_index in range(N_SECTION)]
    grad_sums = [jnp.zeros((N_TENSOR, N_DP, HCAP, BLK, BLK), jnp.float32) for layer_index in range(N_SECTION)]
    for turn in range(TURNS):
        for layer_index in range(N_SECTION):
            if turn == 0:
                grads_in = grad_outputs[layer_index]
            elif layer_index == N_SECTION - 1:
                grads_in = jnp.where((row_ids < live_rows[turn - 1])[:, None], arriving[turn - 1], jnp.zeros_like(arriving[turn - 1]))
            else:
                grads_in = backward_table[layer_index + 1][turn - 1]
            result, block_grads = layer_backward(stashed_inputs[layer_index, turn], grads_in, norm_gain[layer_index], up_weight[layer_index], down_weight[layer_index], held_blocks[layer_index])
            backward_table[layer_index][turn] = result
            grad_sums[layer_index] = grad_sums[layer_index] + block_grads
    first_list = []
    second_list = []
    direction_list = []
    for layer_index in range(N_SECTION):
        owned_grads, is_filled = route_blocks(grad_sums[layer_index], held_count[layer_index], held_owner[layer_index])
        filled = is_filled[..., None, None]
        first_new = 0.9 * first_moment[layer_index] + 0.1 * owned_grads
        second_new = 0.999 * second_moment[layer_index] + 0.001 * owned_grads * owned_grads
        direction = first_new / (jnp.sqrt(second_new) + 1e-08)
        first_list.append(jnp.where(filled, first_new, 0.0))
        second_list.append(jnp.where(filled, second_new, 0.0))
        direction_list.append(jnp.where(filled, direction, 0.0))
    section_outputs = jnp.stack([jnp.stack(forward_table[layer_index]) for layer_index in range(N_SECTION)])
    input_grads = jnp.stack([jnp.stack(backward_table[layer_index]) for layer_index in range(N_SECTION)])
    return (section_outputs, input_grads, jnp.stack(first_list), jnp.stack(second_list), jnp.stack(direction_list))
```

```python
import functools

import jax
import jax.numpy as jnp
from jax import lax
from jax.experimental import pallas as pl
from jax.experimental.pallas import tpu as pltpu
from jax.sharding import PartitionSpec as P

BLK = 128
EPSILON = 1e-06
BF16 = jnp.bfloat16
F32 = jnp.float32


def tensor_sum(value):
    step = 1
    while step < lax.axis_size("tensor"):
        pairs = [(t, t ^ step) for t in range(lax.axis_size("tensor"))]
        value = value + lax.ppermute(value.astype(BF16), "tensor", pairs).astype(F32)
        step *= 2
    return value


def sibling(value):
    return lax.ppermute(value, "dp", [(d, d ^ 1) for d in range(lax.axis_size("dp"))])


def shifted(value, steps):
    count = lax.axis_size("dp")
    return lax.ppermute(value, "dp", [(d, (d + 2 * steps) % count) for d in range(count)])


def gather_rows(local):
    depth = lax.axis_size("dp") // 2
    mine = jnp.stack([local] + [shifted(local, k) for k in range(1, depth)], axis=-3)
    both = jnp.stack([mine, sibling(mine)], axis=-4)
    return both.reshape(local.shape[:-2] + (2 * depth * local.shape[-2], local.shape[-1]))


def gather_passed(local, direction):
    sections = lax.axis_size("section")
    count = lax.axis_size("dp")
    depth = count // 2

    def moved(k):
        pairs = [
            (s * count + d, (s + direction) * count + (d + 2 * k) % count)
            for s in range(sections)
            if 0 <= s + direction < sections
            for d in range(count)
        ]
        return lax.ppermute(local, ("section", "dp"), pairs)

    mine = jnp.stack([moved(k) for k in range(depth)])
    both = jnp.stack([mine, sibling(mine)])
    return both.reshape((2 * depth * local.shape[0], local.shape[1]))


def scatter_rows(partial):
    depth = lax.axis_size("dp") // 2
    slots = partial.reshape((2, depth, partial.shape[0] // (2 * depth), partial.shape[1]))
    pairs = slots[0] + sibling(slots[1].astype(BF16)).astype(F32)
    total = pairs[0]
    for k in range(1, depth):
        total = total + shifted(pairs[k].astype(BF16), -k).astype(F32)
    return total


def split_squares(squares):
    high = squares.astype(BF16)
    low = (squares - high.astype(F32)).astype(BF16)
    lane = lax.broadcasted_iota(jnp.int32, (squares.shape[0], BLK), 1)
    return jnp.where(lane == 0, high[:, None], jnp.where(lane == 1, low[:, None], jnp.zeros((), BF16)))


def normed_product(rows_all, gain_row, up_matrix, width):
    widened = rows_all.astype(F32)
    squares = jnp.sum(widened * widened, axis=1)
    normed = (widened * gain_row.astype(F32)).astype(BF16)
    product = jnp.dot(normed, up_matrix, preferred_element_type=F32)
    step = 1
    while step < lax.axis_size("tensor"):
        pairs = [(t, t ^ step) for t in range(lax.axis_size("tensor"))]
        sent = jnp.concatenate([product.astype(BF16), split_squares(squares)], axis=1)
        got = lax.ppermute(sent, "tensor", pairs).astype(F32)
        hidden_count = product.shape[1]
        product = product + got[:, :hidden_count]
        squares = squares + got[:, hidden_count] + got[:, hidden_count + 1]
        step *= 2
    return normed, product, lax.rsqrt(squares / width + EPSILON)


def activate(hidden):
    return (hidden * jax.nn.sigmoid(hidden)).astype(BF16)


def times_transposed(left, right):
    return lax.dot_general(left, right, (((1,), (1,)), ((), ())), preferred_element_type=F32)


def block_kernel(plan, *refs):
    turns = (len(refs) - 1) // 4
    out = refs[-1]
    slot = pl.program_id(0)
    is_up = plan[0, slot]
    left = pl.ds(pl.multiple_of(plan[1, slot] * BLK, BLK), BLK)
    right = pl.ds(pl.multiple_of(plan[2, slot] * BLK, BLK), BLK)

    def write(left_index, right_index):
        total = jnp.zeros((BLK, BLK), F32)
        for turn in range(turns):
            group = refs[4 * turn : 4 * turn + 4]
            total += lax.dot_general(
                group[left_index][:, left],
                group[right_index][:, right],
                (((0,), (0,)), ((), ())),
                preferred_element_type=F32,
            )
        out[0] = total.astype(BF16)

    @pl.when(is_up == 1)
    def _():
        write(0, 1)

    @pl.when(is_up == 0)
    def _():
        write(2, 3)


def outgoing_blocks(plan, tables):
    slots = plan.shape[1]
    flat = [table for turn in tables for table in turn]
    return pl.pallas_call(
        block_kernel,
        grid_spec=pltpu.PrefetchScalarGridSpec(
            num_scalar_prefetch=1,
            grid=(slots,),
            in_specs=[pl.BlockSpec(table.shape, lambda i, plan: (0, 0)) for table in flat],
            out_specs=pl.BlockSpec((1, BLK, BLK), lambda i, plan: (i, 0, 0)),
        ),
        out_shape=jax.ShapeDtypeStruct((slots, BLK, BLK), BF16),
        compiler_params=pltpu.CompilerParams(vmem_limit_bytes=24 * 1024 * 1024),
        name="block_grads",
    )(plan, *flat)


def adam_kernel(plan, arrived, first, second, first_out, second_out, direction_out):
    slot = pl.program_id(0)
    filled = plan[0, slot] == 1

    @pl.when(filled)
    def _():
        grad = arrived[0].astype(F32)
        first_new = 0.9 * first[0] + 0.1 * grad
        second_new = 0.999 * second[0] + 0.001 * grad * grad
        first_out[0] = first_new
        second_out[0] = second_new
        direction_out[0] = first_new / (jnp.sqrt(second_new) + 1e-08)

    @pl.when(jnp.logical_not(filled))
    def _():
        zeros = jnp.zeros((BLK, BLK), F32)
        first_out[0] = zeros
        second_out[0] = zeros
        direction_out[0] = zeros


def adam(plan, arrived, first, second):
    slots = first.shape[0]
    block = pl.BlockSpec((1, BLK, BLK), lambda i, plan: (i, 0, 0))
    shape = jax.ShapeDtypeStruct((slots, BLK, BLK), F32)
    return pl.pallas_call(
        adam_kernel,
        grid_spec=pltpu.PrefetchScalarGridSpec(
            num_scalar_prefetch=1,
            grid=(slots,),
            in_specs=[pl.BlockSpec((1, BLK, BLK), lambda i, plan: (plan[1, i], 0, 0)), block, block],
            out_specs=[block] * 3,
        ),
        out_shape=[shape] * 3,
        name="adam_step",
    )(plan, arrived, first, second)


def body(
    section_inputs,
    entering,
    grad_outputs,
    arriving,
    live_rows,
    stashed_inputs,
    norm_gain,
    up_weight,
    down_weight,
    held_blocks,
    held_count,
    held_owner,
    first_moment,
    second_moment,
):
    section_count = lax.axis_size("section")
    section_index = lax.axis_index("section")
    dp_index = lax.axis_index("dp")
    dp_count = lax.axis_size("dp")
    depth = dp_count // 2
    turn_count = stashed_inputs.shape[1]
    local_rows = section_inputs.shape[1]
    gain_row = norm_gain[0]
    up_matrix = up_weight[0]
    down_matrix = down_weight[0]
    channels = up_matrix.shape[0]
    width = channels * lax.axis_size("tensor")
    channel_blocks = channels // BLK
    hidden_blocks = up_matrix.shape[1] // BLK
    up_count = channel_blocks * hidden_blocks
    is_first = section_index == 0
    is_last = section_index == section_count - 1
    row_ids = dp_index * local_rows + lax.iota(jnp.int32, local_rows)

    start_grads = grad_outputs[0]
    later_inputs = []
    for turn in range(1, turn_count):
        live = (row_ids < live_rows[turn - 1])[:, None]
        masked = jnp.where(live, arriving[turn - 1], jnp.zeros((), BF16))
        later_inputs.append(jnp.where(is_last, masked, entering[turn - 1]))
    first_pair = gather_rows(jnp.stack([stashed_inputs[0, 0], start_grads]))
    others = gather_rows(jnp.stack([section_inputs[0]] + [stashed_inputs[0, u] for u in range(1, turn_count)] + later_inputs))
    stash_all = [first_pair[0]] + [others[u] for u in range(1, turn_count)]
    edge_all = [others[turn_count - 1 + u] for u in range(1, turn_count)]

    forward_results = []
    backward_results = []
    tables = []
    for turn in range(turn_count):
        if turn == 0:
            grads_in, grads_all = start_grads, first_pair[1]
        else:
            passed = gather_passed(backward_results[-1], -1)
            grads_all = jnp.where(is_last, edge_all[turn - 1], passed)
            grads_in = jnp.where(is_last, later_inputs[turn - 1], passed[:local_rows])
        rows_local = stashed_inputs[0, turn]
        normed, product, row_scales = normed_product(stash_all[turn], gain_row, up_matrix, width)
        act_grad = tensor_sum(times_transposed(grads_all, down_matrix))
        hidden = product * row_scales[:, None]
        gate = jax.nn.sigmoid(hidden)
        activated = (hidden * gate).astype(BF16)
        hidden_grad = act_grad * gate * (1.0 + hidden * (1.0 - gate))
        scaled_grad = (hidden_grad * row_scales[:, None]).astype(BF16)
        scale_grad = jnp.sum(hidden_grad * product, axis=1)
        normed_part = times_transposed(scaled_grad, up_matrix)
        widened_all = stash_all[turn].astype(F32)
        input_part = (
            normed_part * gain_row.astype(F32)
            - (scale_grad * row_scales**3 / width)[:, None] * widened_all
        )
        input_grad = grads_in.astype(F32) + scatter_rows(input_part)
        backward_results.append(input_grad.astype(BF16))
        tables.append((normed, scaled_grad, activated, grads_all))
        if turn == 0:
            rows_in, rows_all = section_inputs[0], others[0]
        else:
            passed = gather_passed(forward_results[-1], 1)
            rows_all = jnp.where(is_first, edge_all[turn - 1], passed)
            rows_in = jnp.where(is_first, later_inputs[turn - 1], passed[:local_rows])
        _, product, row_scales = normed_product(rows_all, gain_row, up_matrix, width)
        forward_activated = activate(product * row_scales[:, None])
        mixed = scatter_rows(jnp.dot(forward_activated, down_matrix, preferred_element_type=F32))
        forward_results.append((rows_in.astype(F32) + mixed).astype(BF16))

    counts = held_count[0, 0]
    owners = held_owner[0, 0]
    capacity = owners.shape[1]
    slot_ids = lax.iota(jnp.int32, capacity)
    dp_ids = lax.iota(jnp.int32, dp_count)
    live_slots = slot_ids[None, :] < counts[:, None]
    chosen = (owners[:, None, :] == dp_ids[None, :, None]) & live_slots[:, None, :]
    is_sent = jnp.any(chosen, axis=2)
    my_z, my_core = dp_index // 2, dp_index % 2
    slots = lax.iota(jnp.int32, dp_count)
    slot_owner = 2 * ((my_z - slots % depth) % depth) + (my_core + slots // depth) % 2
    my_owners = lax.dynamic_index_in_dim(owners, dp_index, 0, keepdims=False)
    my_count = lax.dynamic_index_in_dim(counts, dp_index, 0, keepdims=False)
    my_blocks = lax.dynamic_index_in_dim(held_blocks[0, 0], dp_index, 0, keepdims=False)
    to_slot = (my_owners[None, :] == slot_owner[:, None]) & (slot_ids < my_count)[None, :]
    number = jnp.sum(jnp.where(to_slot, my_blocks[None, :], 0), axis=1)
    is_up = number < up_count
    down_number = number - up_count
    left_index = jnp.where(is_up, number // hidden_blocks, down_number // channel_blocks)
    right_index = jnp.where(is_up, number % hidden_blocks, down_number % channel_blocks)
    plan = jnp.stack([is_up.astype(jnp.int32), left_index, right_index])

    outgoing = outgoing_blocks(plan, tables).reshape((2, depth, BLK, BLK))
    relayed = sibling(outgoing[1])
    both = jnp.stack([outgoing[0], relayed], axis=1)
    arrived = jnp.concatenate([both[:1]] + [shifted(both[k], -k)[None] for k in range(1, depth)])
    arrived = arrived.reshape((dp_count, BLK, BLK))

    from_source = lax.dynamic_index_in_dim(is_sent, dp_index, 1, keepdims=False)
    source_count = from_source.astype(jnp.int32)
    ranks = jnp.cumsum(source_count) - source_count
    matches = from_source[None, :] & (ranks[None, :] == slot_ids[:, None])
    source_place = 2 * ((dp_ids // 2 - my_z) % depth) + (dp_ids + my_core) % 2
    arrived_index = jnp.sum(jnp.where(matches, source_place[None, :], 0), axis=1)
    adam_plan = jnp.stack([jnp.any(matches, axis=1).astype(jnp.int32), arrived_index])
    first_out, second_out, direction_out = adam(adam_plan, arrived, first_moment[0, 0, 0], second_moment[0, 0, 0])
    return (
        jnp.stack(forward_results)[None],
        jnp.stack(backward_results)[None],
        first_out[None, None, None],
        second_out[None, None, None],
        direction_out[None, None, None],
    )


def solution(mesh):
    return jax.shard_map(
        body,
        mesh=mesh,
        in_specs=(
            P("section", "dp", "tensor"),
            P(None, "dp", "tensor"),
            P("section", "dp", "tensor"),
            P(None, "dp", "tensor"),
            P(),
            P("section", None, "dp", "tensor"),
            P("section", "tensor"),
            P("section", "tensor", "dp"),
            P("section", "dp", "tensor"),
            P("section", "tensor", None, None),
            P("section", "tensor", None),
            P("section", "tensor", None, None),
            P("section", "tensor", "dp", None, None, None),
            P("section", "tensor", "dp", None, None, None),
        ),
        out_specs=(
            P("section", None, "dp", "tensor"),
            P("section", None, "dp", "tensor"),
            P("section", "tensor", "dp", None, None, None),
            P("section", "tensor", "dp", None, None, None),
            P("section", "tensor", "dp", None, None, None),
        ),
        check_vma=False,
    )
```

```python
import functools

import jax
import jax.numpy as jnp
from jax import lax
from jax.experimental import pallas as pl
from jax.experimental.pallas import tpu as pltpu
from jax.sharding import PartitionSpec as P

BLK = 128
EPSILON = 1e-06
BF16 = jnp.bfloat16
F32 = jnp.float32
MIB = 1024 * 1024
VMEM = pl.BlockSpec(memory_space=pltpu.VMEM)
SMEM = pl.BlockSpec(memory_space=pltpu.SMEM)
HBM = pl.BlockSpec(memory_space=pltpu.HBM)
ANY = pl.BlockSpec(memory_space=pl.ANY)
DP, COUNT, OWNERS = range(3)


def later(values, *before):
    return lax.optimization_barrier((values, before))[0]


def sibling(value):
    return lax.ppermute(value, "dp", [(d, d ^ 1) for d in range(lax.axis_size("dp"))])


def shifted(value, steps):
    count = lax.axis_size("dp")
    return lax.ppermute(value, "dp", [(d, (d + 2 * steps) % count) for d in range(count)])


def moved_rows(local):
    depth = lax.axis_size("dp") // 2
    return [local] + [shifted(local, k) for k in range(1, depth)]


def moved_passed(down, up=None):
    sections = lax.axis_size("section")
    count = lax.axis_size("dp")

    def moved(local, direction, k):
        pairs = [
            (s * count + d, (s + direction) % sections * count + (d + 2 * k) % count)
            for s in range(sections)
            for d in range(count)
        ]
        return lax.ppermute(local, ("section", "dp"), pairs)

    both = down[None] if up is None else jnp.stack([down, up])
    if sections == 2:
        return [moved(both, 1, k) for k in range(count // 2)]
    return [jnp.stack([moved(down, -1, k), moved(up, 1, k)]) for k in range(count // 2)]


def halves(pieces):
    mine = jnp.concatenate(pieces, axis=-2)
    return mine, sibling(mine)


def scatter_pairs(kept, sent):
    depth = lax.axis_size("dp") // 2
    return (kept + sibling(sent).astype(F32)).reshape((depth, kept.shape[0] // depth, kept.shape[1]))


def scatter_parts(pairs):
    return [pairs[0]] + [shifted(pairs[k].astype(BF16), -k) for k in range(1, pairs.shape[0])]


def added(rows, parts):
    return sum([part.astype(F32) for part in parts], rows.astype(F32)).astype(BF16)


def tensor_parts(value):
    count = lax.axis_size("tensor")
    step = 1
    while True:
        got = lax.ppermute(value, "tensor", [(t, t ^ step) for t in range(count)])
        step *= 2
        if step >= count:
            return value, got
        value = value + got


def tile_of(size):
    return 256 if size % 256 == 0 else BLK


def call(kernel, name, outs, operands, specs, flops, moved, scratch=()):
    return pl.pallas_call(
        kernel,
        out_shape=outs,
        in_specs=specs,
        out_specs=[VMEM] * len(outs),
        scratch_shapes=scratch,
        compiler_params=pltpu.CompilerParams(vmem_limit_bytes=12 * MIB),
        cost_estimate=pl.CostEstimate(flops=flops, bytes_accessed=moved, transcendentals=0),
        name=name,
    )(*operands)


def struct(*shape, dtype=BF16):
    return jax.ShapeDtypeStruct(shape, dtype)


def nt_dot(left, right):
    return lax.dot_general(left, right, (((1,), (1,)), ((), ())), preferred_element_type=F32)


def load_kernel(up_in, down_in, after, up, down, sems):
    copies = [pltpu.make_async_copy(up_in, up, sems.at[0]), pltpu.make_async_copy(down_in, down, sems.at[1])]
    for copy in copies:
        copy.start()
    for copy in copies:
        copy.wait()


def load_weights(up, down, after):
    return pl.pallas_call(
        load_kernel,
        out_shape=[pltpu.VMEM(up.shape, BF16), pltpu.VMEM(down.shape, BF16)],
        in_specs=[HBM] * 2 + [ANY],
        out_specs=[VMEM] * 2,
        scratch_shapes=[pltpu.SemaphoreType.DMA((2,))],
        compiler_params=pltpu.CompilerParams(vmem_limit_bytes=16 * MIB),
        name="load_weights",
    )(in_hbm(up), in_hbm(down), after)


def in_hbm(value):
    return pltpu.with_memory_space_constraint(value, pltpu.HBM)


def write_products(rows, gain, up, sent, normed):
    widened = rows.astype(F32)
    squares = jnp.sum(widened * widened, axis=1, keepdims=True)
    normed[...] = (widened * gain[...].astype(F32)).astype(BF16)
    hidden = up.shape[1]
    step = tile_of(hidden)
    for n in range(0, hidden, step):
        sent[:, n : n + step] = jnp.dot(normed[...], up[:, n : n + step], preferred_element_type=F32).astype(BF16)
    coarse = squares.astype(BF16).astype(F32)
    lane = lax.broadcasted_iota(jnp.int32, (rows.shape[0], BLK), 1)
    sent[:, hidden:] = jnp.where(lane == 0, coarse, jnp.where(lane == 1, squares - coarse, 0.0)).astype(BF16)


def write_act_grads(grads, down, sent):
    hidden = down.shape[0]
    step = tile_of(hidden)
    for n in range(0, hidden, step):
        sent[:, n : n + step] = nt_dot(grads[...], down[n : n + step, :]).astype(BF16)


def joined(low, high):
    return jnp.concatenate([low[...], high[...]], axis=0)


def product_kernel(low, high, gain, up, _, sent, normed):
    write_products(joined(low, high), gain, up, sent, normed)


def products(row_halves, gain, up, down):
    rows = 2 * row_halves[0].shape[0]
    channels, hidden = up.shape
    return call(
        product_kernel, "products", [struct(rows, hidden + BLK)],
        [*row_halves, gain, up, down], [VMEM] * 5, 2 * rows * channels * hidden, 2 * channels * hidden,
        [pltpu.VMEM((rows, channels), BF16)],
    )[0]


def act_kernel(low, high, down, _, sent, grads):
    grads[...] = joined(low, high)
    write_act_grads(grads, down, sent)


def act_grads(grad_halves, up, down):
    rows = 2 * grad_halves[0].shape[0]
    hidden, channels = down.shape
    return call(
        act_kernel, "act_grads", [struct(rows, hidden)],
        [*grad_halves, down, up], [VMEM] * 4, 2 * rows * channels * hidden, 2 * channels * hidden,
        [pltpu.VMEM((rows, channels), BF16)],
    )[0]


def scales_in(own, got, hidden, width):
    tail = own[:, hidden:].astype(F32) + got[:, hidden:].astype(F32)
    return lax.rsqrt((tail[:, 0:1] + tail[:, 1:2]) / width + EPSILON)


def gate_of(hidden):
    return 1.0 / (1.0 + jnp.exp(-hidden))


def write_backward(width, own, got, act_own, act_got, low, high, gain, up, kept, sent, scaled, activated):
    channels, hidden = up.shape
    scales = scales_in(own, got, hidden, width)
    scale_grad = jnp.zeros_like(scales)
    step = tile_of(hidden)
    for n in range(0, hidden, step):
        cut = slice(n, n + step)
        product = own[:, cut].astype(F32) + got[:, cut].astype(F32)
        act_grad = act_own[:, cut].astype(F32) + act_got[:, cut].astype(F32)
        value = product * scales
        gate = gate_of(value)
        activated[:, cut] = (value * gate).astype(BF16)
        grad = act_grad * gate * (1.0 + value * (1.0 - gate))
        scaled[:, cut] = (grad * scales).astype(BF16)
        scale_grad += jnp.sum(grad * product, axis=1, keepdims=True)
    factor = scale_grad * scales * scales * scales / width
    half = low.shape[0]
    step = tile_of(channels)
    for c in range(0, channels, step):
        cut = slice(c, c + step)
        part = nt_dot(scaled[...], up[cut, :]) * gain[:, cut].astype(F32)
        kept[:, cut] = part[:half] - factor[:half] * low[:, cut].astype(F32)
        sent[:, cut] = (part[half:] - factor[half:] * high[:, cut].astype(F32)).astype(BF16)


def write_forward(width, own, got, down, kept, sent, activated):
    hidden, channels = down.shape
    scales = scales_in(own, got, hidden, width)
    step = tile_of(hidden)
    for n in range(0, hidden, step):
        cut = slice(n, n + step)
        value = (own[:, cut].astype(F32) + got[:, cut].astype(F32)) * scales
        activated[:, cut] = (value * gate_of(value)).astype(BF16)
    half = kept.shape[0]
    step = tile_of(channels)
    for c in range(0, channels, step):
        cut = slice(c, c + step)
        part = jnp.dot(activated[...], down[:, cut], preferred_element_type=F32)
        kept[:, cut] = part[:half]
        sent[:, cut] = part[half:].astype(BF16)


def backward_kernel(width, own, got, act_own, act_got, low, high, gain, up, _, *refs):
    write_backward(width, own, got, act_own, act_got, low, high, gain, up, *refs[-4:])


def backward(width, products_parts, act_parts, row_halves, gain, up, down, after):
    half, channels = row_halves[0].shape
    hidden = up.shape[1]
    outs = [struct(half, channels, dtype=F32), struct(half, channels), struct(2 * half, hidden), struct(2 * half, hidden)]
    operands = [*products_parts, *act_parts, *row_halves, gain, up, down]
    return call(
        functools.partial(backward_kernel, width), "backward", outs, operands + after,
        [VMEM] * len(operands) + [ANY] * len(after),
        4 * half * channels * hidden, 2 * channels * hidden,
    )


def forward_kernel(width, own, got, down, _, *refs):
    write_forward(width, own, got, down, *refs[-3:])


def forward(width, products_parts, up, down, after):
    rows = products_parts[0].shape[0]
    hidden, channels = down.shape
    outs = [struct(rows // 2, channels, dtype=F32), struct(rows // 2, channels)]
    return call(
        functools.partial(forward_kernel, width), "forward", outs, [*products_parts, down, up, *after],
        [VMEM] * 4 + [ANY] * len(after),
        2 * rows * channels * hidden, 2 * channels * hidden, [pltpu.VMEM((rows, hidden), BF16)],
    )


def enter_kernel(flag, low, high, other_low, other_high, gain, up, down, sent, grads, normed):
    @pl.when(flag[0] == 1)
    def _():
        write_products(joined(low, high), gain, up, sent, normed)
        grads[...] = joined(other_low, other_high)

    @pl.when(flag[0] == 0)
    def _():
        grads[...] = joined(low, high)
        write_act_grads(grads, down, sent)
        sent[:, up.shape[1] :] = jnp.zeros((sent.shape[0], BLK), BF16)


def enter(flag, row_halves, other_halves, gain, up, down):
    rows = 2 * row_halves[0].shape[0]
    channels, hidden = up.shape
    return call(
        enter_kernel, "enter", [struct(rows, hidden + BLK), struct(rows, channels)],
        [flag, *row_halves, *other_halves, gain, up, down], [SMEM] + [VMEM] * 7,
        2 * rows * channels * hidden, 2 * channels * hidden, [pltpu.VMEM((rows, channels), BF16)],
    )


def leave_kernel(width, flag, own, got, back_own, back_got, low, high, gain, up, down, *refs):
    kept, sent, scaled, activated, scratch = refs[-5:]

    @pl.when(flag[0] == 1)
    def _():
        write_forward(width, own, got, down, kept, sent, scratch)

    @pl.when(flag[0] == 0)
    def _():
        write_backward(width, back_own, back_got, own, got, low, high, gain, up, kept, sent, scaled, activated)


def leave(width, flag, parts, back_parts, row_halves, gain, up, down, filled, after):
    half, channels = row_halves[0].shape
    hidden = up.shape[1]
    outs = [struct(half, channels, dtype=F32), struct(half, channels), struct(2 * half, hidden), struct(2 * half, hidden)]
    operands = [flag, *parts, *back_parts, *row_halves, gain, up, down, *filled]
    first = len(operands) - len(filled)
    return pl.pallas_call(
        functools.partial(leave_kernel, width),
        out_shape=outs,
        in_specs=[SMEM] + [VMEM] * (len(operands) - 1) + [ANY] * len(after),
        out_specs=[VMEM] * 4,
        scratch_shapes=[pltpu.VMEM((2 * half, hidden), BF16)],
        input_output_aliases={first + i: 2 + i for i in range(len(filled))},
        compiler_params=pltpu.CompilerParams(vmem_limit_bytes=12 * MIB),
        cost_estimate=pl.CostEstimate(flops=4 * half * channels * hidden, bytes_accessed=2 * channels * hidden, transcendentals=0),
        name="leave",
    )(*operands, *after)


def block_kernel(channel_blocks, hidden_blocks, depth, capacity, table_counts, plan, gain, *refs):
    *tables, out = refs
    up_count = channel_blocks * hidden_blocks
    dp_index = plan[0, DP]
    z, core = dp_index // 2, lax.rem(dp_index, 2)

    def per_slot(slot, carry):
        owner = 2 * lax.rem(z - lax.rem(slot, depth) + depth, depth) + lax.rem(core + slot // depth, 2)
        number = jnp.int32(-1)
        for entry in range(capacity):
            here = jnp.logical_and(plan[dp_index, OWNERS + entry] == owner, entry < plan[dp_index, COUNT])
            number = jnp.where(here, plan[dp_index, OWNERS + capacity + entry], number)
        is_up = number < up_count
        down_number = jnp.maximum(number - up_count, 0)
        up_number = jnp.maximum(number, 0)
        left_index = jnp.where(is_up, up_number // hidden_blocks, down_number // channel_blocks)
        right_index = jnp.where(is_up, lax.rem(up_number, hidden_blocks), lax.rem(down_number, channel_blocks))
        left = pl.ds(pl.multiple_of(left_index * BLK, BLK), BLK)
        right = pl.ds(pl.multiple_of(right_index * BLK, BLK), BLK)

        def both(halves, cut):
            return jnp.concatenate([half[:, cut] for half in halves], axis=0)

        groups = []
        start = 0
        for count in table_counts:
            groups.append(tables[start : start + count])
            start += count

        def write(is_up_block):
            total = jnp.zeros((BLK, BLK), F32)
            for group in groups:
                rows, scaled, activated, grads = group[:2], group[2], group[3], group[4:]
                if is_up_block:
                    first = (both(rows, left).astype(F32) * gain[:, left].astype(F32)).astype(BF16)
                    second = scaled[:, right]
                else:
                    first = activated[:, left]
                    second = both(grads, right)
                total += lax.dot_general(first, second, (((0,), (0,)), ((), ())), preferred_element_type=F32)
            out[slot] = total.astype(BF16)

        @pl.when(jnp.logical_and(number >= 0, is_up))
        def _():
            write(True)

        @pl.when(jnp.logical_not(is_up))
        def _():
            write(False)

        @pl.when(number < 0)
        def _():
            out[slot] = jnp.zeros((BLK, BLK), BF16)

        return carry

    lax.fori_loop(0, out.shape[0], per_slot, 0)


def outgoing_blocks(plan, capacity, gain, tables, channel_blocks, hidden_blocks):
    slots = lax.axis_size("dp")
    flat = [table for turn in tables for table in turn]
    kernel = functools.partial(
        block_kernel, channel_blocks, hidden_blocks, slots // 2, capacity, [len(turn) for turn in tables]
    )
    return call(
        kernel, "block_grads", [struct(slots, BLK, BLK)], [plan, gain, *flat],
        [SMEM, VMEM] + [VMEM] * len(flat), 4 * slots * BLK * BLK * BLK, 2 * slots * BLK * BLK,
    )[0]


def adam_kernel(depth, plan, relayed, *refs):
    *others, first, second, first_out, second_out, direction_out = refs
    dp_index = plan[0, DP]
    z, core = dp_index // 2, lax.rem(dp_index, 2)
    slots, capacity = plan.shape[0], first.shape[0]
    first_out[...] = jnp.zeros(first_out.shape, F32)
    second_out[...] = jnp.zeros(first_out.shape, F32)
    direction_out[...] = jnp.zeros(first_out.shape, F32)

    def update(place, grad):
        grad = grad.astype(F32)
        first_new = 0.9 * first[place] + 0.1 * grad
        second_new = 0.999 * second[place] + 0.001 * grad * grad
        first_out[place] = first_new
        second_out[place] = second_new
        direction_out[place] = first_new / (jnp.sqrt(second_new) + 1e-08)

    def per_source(source, place):
        sends = False
        for entry in range(capacity):
            sends = jnp.logical_or(sends, jnp.logical_and(plan[source, OWNERS + entry] == dp_index, entry < plan[source, COUNT]))
        back = lax.rem(source // 2 - z + depth, depth)
        across = lax.rem(source + core, 2)
        for k in range(depth):
            @pl.when(jnp.logical_and(sends, back == k))
            def _():
                if k == 0:
                    update(place, relayed[0])
                else:
                    update(place, others[k - 1][across])

        return place + jnp.where(sends, 1, 0)

    lax.fori_loop(0, slots, per_source, 0)


def adam(plan, relayed, others, first, second):
    shape = jax.ShapeDtypeStruct(first.shape, F32)
    operands = [plan, relayed, *others, first, second]
    return call(
        functools.partial(adam_kernel, lax.axis_size("dp") // 2), "adam_step", [shape] * 3, operands,
        [SMEM] + [VMEM] * (len(operands) - 1), 20 * first.size, 20 * first.size,
    )


def finish_kernel(earlier_count, *refs):
    earlier, rows, parts, out = refs[:earlier_count], refs[earlier_count], refs[earlier_count + 1 : -1], refs[-1]
    for turn in range(earlier_count):
        out[turn] = earlier[turn][...]
    total = rows[...].astype(F32)
    for part in parts:
        total += part[...].astype(F32)
    out[earlier_count] = total.astype(BF16)


def finish(earlier, rows, parts):
    operands = [*earlier, rows, *parts]
    return call(
        functools.partial(finish_kernel, len(earlier)), "finish", [struct(len(earlier) + 1, *rows.shape)], operands,
        [VMEM] * len(operands), rows.size, 8 * rows.size,
    )[0]


def finish_pair_kernel(depth, flag, chained, off_back, forward_rows, chain_rows, *refs):
    forward_parts, chain_parts, (section_out, grads_out) = refs[:depth], refs[depth : 2 * depth], refs[2 * depth :]

    def total(rows, parts):
        value = rows[...].astype(F32)
        for part in parts:
            value += part[...].astype(F32)
        return value.astype(BF16)

    off_forward = total(forward_rows, forward_parts)
    chained_later = total(chain_rows, chain_parts)

    @pl.when(flag[0] == 1)
    def _():
        section_out[0] = chained[...]
        section_out[1] = off_forward
        grads_out[0] = off_back[...]
        grads_out[1] = chained_later

    @pl.when(flag[0] == 0)
    def _():
        section_out[0] = off_forward
        section_out[1] = chained_later
        grads_out[0] = chained[...]
        grads_out[1] = off_back[...]


def finish_pair(flag, chained, off_back, forward_rows, forward_parts, chain_rows, chain_parts):
    operands = [flag, chained, off_back, forward_rows, chain_rows, *forward_parts, *chain_parts]
    return call(
        functools.partial(finish_pair_kernel, len(chain_parts)), "finish_pair", [struct(2, *chained.shape)] * 2, operands,
        [SMEM] + [VMEM] * (len(operands) - 1), 8 * chained.size, 16 * chained.size,
    )


def relay_pair(
    is_first, masked, entering, begin, start, stash, gain, up, down, width
):
    def pick(first, last):
        return jnp.where(is_first, first, last)

    flag = pick(jnp.int32(1), jnp.int32(0)).reshape(1)
    other_flag = 1 - flag
    chain_in = pick(begin, start)
    first = jnp.stack([pick(stash[1], stash[0]), chain_in])
    off_grads, off_rows = pick(start, masked[0]), pick(entering[0], begin)
    others = jnp.stack([pick(stash[0], stash[1]), off_grads, off_rows])
    up, down, flag, other_flag, others = lax.optimization_barrier((up, down, flag, other_flag, others))

    with jax.named_scope("gather_first"):
        moved = moved_rows(first)
    up, down = load_weights(up, down, first)
    with jax.named_scope("gather_first"):
        gathered = halves(later(moved, up))
    back_halves, chain_halves = [[half[i] for half in gathered] for i in range(2)]
    back_product = products(back_halves, gain, up, down)
    with jax.named_scope("swap_back"):
        back_parts = tensor_parts(back_product)
    entered, _ = enter(flag, later(chain_halves, back_product), chain_halves, gain, up, down)
    with jax.named_scope("swap_chain0"):
        parts = tensor_parts(entered)
    with jax.named_scope("gather_others"):
        gathered = halves(later(moved_rows(later(others, entered)), back_parts[1]))
    off_halves, off_grad_halves, off_row_halves = [[half[i] for half in gathered] for i in range(3)]
    off_product = products(off_halves, gain, up, down)
    with jax.named_scope("swap_off_back"):
        off_parts = tensor_parts(off_product)
    off_act = act_grads(later(off_grad_halves, off_product), up, down)
    with jax.named_scope("swap_off_act"):
        off_act_parts = tensor_parts(off_act)
    off_forward = products(later(off_row_halves, off_act), gain, up, down)

    with jax.named_scope("chain0"):
        kept, sent, scaled, activated = leave(
            width, flag, parts, back_parts, back_halves, gain, up, down, [], [off_product, off_act, off_forward]
        )
        sums = scatter_parts(scatter_pairs(kept, sent))
        chained = added(chain_in, later(sums, off_parts[1]))
    with jax.named_scope("pass"):
        passed = halves([one[0] for one in moved_passed(chained)])
    chain_in = passed[0][: chained.shape[0]]
    entered, grads = enter(other_flag, later(passed, off_act_parts[1]), chain_halves, gain, up, down)
    with jax.named_scope("swap_chain1"):
        parts = tensor_parts(entered)
    with jax.named_scope("off_back"):
        kept, sent, off_scaled, off_activated = backward(
            width, off_parts, off_act_parts, off_halves, gain, up, down, [entered]
        )
        off_back_sums = scatter_parts(scatter_pairs(kept, sent))
    with jax.named_scope("swap_off_forward"):
        off_forward_parts = tensor_parts(later(off_forward, entered))
    with jax.named_scope("chain1"):
        kept, sent, scaled, activated = leave(
            width, other_flag, parts, back_parts, back_halves, gain, up, down, [scaled, activated], []
        )
        chain_sums = scatter_parts(scatter_pairs(kept, sent))
        off_back = added(off_grads, later(off_back_sums, kept))
    with jax.named_scope("off_forward"):
        kept, sent = forward(width, later(off_forward_parts, chain_sums), up, down, [])
        off_sums = scatter_parts(scatter_pairs(kept, sent))
    section_outputs, input_grads = finish_pair(flag, chained, off_back, off_rows, off_sums, chain_in, chain_sums)
    tables = [
        (*back_halves, scaled, activated, grads),
        (*off_halves, off_scaled, off_activated, *off_grad_halves),
    ]
    return section_outputs, input_grads, tables, off_back


def relay(
    is_first, is_last, masked, entering, section_inputs, grad_outputs, stashed_inputs, gain, up, down, width
):
    turn_count = stashed_inputs.shape[1]
    local_rows = section_inputs.shape[1]
    up, down, is_first, is_last, masked = lax.optimization_barrier((up, down, is_first, is_last, masked))
    grads_in, rows_in = grad_outputs[0], section_inputs[0]
    first = jnp.concatenate([stashed_inputs[0, :1], grad_outputs])
    with jax.named_scope("gather_first"):
        moved = moved_rows(first)
    up, down = load_weights(up, down, first)
    with jax.named_scope("gather_first"):
        gathered = halves(later(moved, up))
    stash_rows = [[half[0] for half in gathered]]
    grad_halves = [half[1] for half in gathered]
    back_products = [products(stash_rows[0], gain, up, down)]
    with jax.named_scope("swap_b0p"):
        back_parts = [tensor_parts(back_products[0])]
    act_grad = act_grads(later(grad_halves, back_products[0]), up, down)
    with jax.named_scope("swap_b0a"):
        act_parts = tensor_parts(act_grad)
    with jax.named_scope("gather_others"):
        others = jnp.concatenate([section_inputs, stashed_inputs[0, 1:]])
        gathered = halves(moved_rows(later(others, act_grad)))
    product = products([half[0] for half in gathered], gain, up, down)
    with jax.named_scope("swap_f0p"):
        parts = tensor_parts(product)
    ahead = [product]
    for turn in range(1, turn_count):
        stash_rows.append([half[turn] for half in gathered])
        back_products.append(products(stash_rows[turn], gain, up, down))
        ahead.append(back_products[turn])
        with jax.named_scope("swap_b1p"):
            back_parts.append(tensor_parts(back_products[turn]))

    forward_results = []
    backward_results = []
    tables = []
    for turn in range(turn_count):
        with jax.named_scope(f"backward{turn}"):
            kept, sent, scaled, activated = backward(
                width, back_parts[turn], act_parts, stash_rows[turn], gain, up, down, ahead
            )
            back_pairs = scatter_pairs(kept, sent)
        tables.append((*stash_rows[turn], scaled, activated, *grad_halves))
        if turn + 1 == turn_count:
            with jax.named_scope(f"backward{turn}"):
                back_sums = scatter_parts(back_pairs)
            parts = later(parts, back_sums)
        with jax.named_scope(f"forward{turn}"):
            kept, sent = forward(width, parts, up, down, [])
            pairs = scatter_pairs(kept, sent)
        if turn + 1 == turn_count:
            with jax.named_scope(f"forward{turn}"):
                sums = scatter_parts(pairs)
            input_grads = finish(backward_results, grads_in, back_sums)
            section_outputs = finish(forward_results, rows_in, sums)
            break
        with jax.named_scope(f"scatter{turn}"):
            sums = scatter_parts(jnp.stack([back_pairs, pairs], axis=1))
        backward_results.append(added(grads_in, [part[0] for part in sums]))
        forward_results.append(added(rows_in, [part[1] for part in sums]))
        with jax.named_scope(f"gather{turn}"):
            moved = moved_passed(
                jnp.where(is_first, masked[turn], backward_results[-1]),
                jnp.where(is_last, entering[turn], forward_results[-1]),
            )
            passed = halves(later(moved, back_parts[turn + 1][1]))
        grad_halves = [half[0] for half in passed]
        grads_in, rows_in = passed[0][0, :local_rows], passed[0][1, :local_rows]
        act_grad = act_grads(grad_halves, up, down)
        with jax.named_scope("swap_b1a"):
            act_parts = tensor_parts(act_grad)
        product = products(later([half[1] for half in passed], act_grad), gain, up, down)
        with jax.named_scope("swap_f1p"):
            parts = tensor_parts(product)
        ahead = []
    return section_outputs, input_grads, tables


def body(
    section_inputs,
    entering,
    grad_outputs,
    arriving,
    live_rows,
    stashed_inputs,
    norm_gain,
    up_weight,
    down_weight,
    held_blocks,
    held_count,
    held_owner,
    first_moment,
    second_moment,
):
    section_count = lax.axis_size("section")
    section_index = lax.axis_index("section")
    dp_count = lax.axis_size("dp")
    turn_count = stashed_inputs.shape[1]
    local_rows = section_inputs.shape[1]
    channels, hidden = up_weight.shape[1:]
    width = channels * lax.axis_size("tensor")
    is_first = section_index == 0
    is_last = section_index == section_count - 1
    counts, owners = held_count[0, 0], held_owner[0, 0]
    capacity = owners.shape[1]
    dp_index = lax.axis_index("dp")
    plan = jnp.concatenate(
        [jnp.full((dp_count, 1), dp_index, jnp.int32), counts[:, None], owners, held_blocks[0, 0]], axis=1
    )
    row_ids = dp_index * local_rows + lax.iota(jnp.int32, local_rows)
    masked = jnp.where((row_ids < live_rows[:, None])[..., None], arriving, jnp.zeros((), BF16))

    if section_count == 2 and turn_count == 2:
        weights = lax.optimization_barrier((up_weight[0], down_weight[0], plan))
        section_outputs, input_grads, tables, before = relay_pair(
            is_first, masked, entering, section_inputs[0], grad_outputs[0], stashed_inputs[0], norm_gain, *weights[:2], width
        )
        plan = later(weights[2], before)
    else:
        section_outputs, input_grads, tables = relay(
            is_first, is_last, masked, entering, section_inputs, grad_outputs, stashed_inputs, norm_gain,
            up_weight[0], down_weight[0], width,
        )
    with jax.named_scope("block_exchange"):
        outgoing = outgoing_blocks(plan, capacity, norm_gain, tables, channels // BLK, hidden // BLK)
        outgoing = outgoing.reshape((2, dp_count // 2, BLK, BLK))
        relayed = sibling(outgoing[1])
        others = [shifted(jnp.stack([outgoing[0, k], relayed[k]]), -k) for k in range(1, dp_count // 2)]
    first_out, second_out, direction_out = adam(plan, relayed, others, first_moment[0, 0, 0], second_moment[0, 0, 0])
    return (
        section_outputs[None],
        input_grads[None],
        first_out[None, None, None],
        second_out[None, None, None],
        direction_out[None, None, None],
    )


def solution(mesh):
    return jax.shard_map(
        body,
        mesh=mesh,
        in_specs=(
            P("section", "dp", "tensor"),
            P(None, "dp", "tensor"),
            P("section", "dp", "tensor"),
            P(None, "dp", "tensor"),
            P(),
            P("section", None, "dp", "tensor"),
            P("section", "tensor"),
            P("section", "tensor", "dp"),
            P("section", "dp", "tensor"),
            P("section", "tensor", None, None),
            P("section", "tensor", None),
            P("section", "tensor", None, None),
            P("section", "tensor", "dp", None, None, None),
            P("section", "tensor", "dp", None, None, None),
        ),
        out_specs=(
            P("section", None, "dp", "tensor"),
            P("section", None, "dp", "tensor"),
            P("section", "tensor", "dp", None, None, None),
            P("section", "tensor", "dp", None, None, None),
            P("section", "tensor", "dp", None, None, None),
        ),
        check_vma=False,
    )
```

```python
import functools

import jax
import jax.numpy as jnp
from jax import lax
from jax.experimental import pallas as pl
from jax.experimental.pallas import tpu as pltpu
from jax.sharding import PartitionSpec as P

BLK = 128
EPSILON = 1e-06
BF16 = jnp.bfloat16
F32 = jnp.float32
MIB = 1024 * 1024
VMEM = pl.BlockSpec(memory_space=pltpu.VMEM)
SMEM = pl.BlockSpec(memory_space=pltpu.SMEM)
HBM = pl.BlockSpec(memory_space=pltpu.HBM)
ANY = pl.BlockSpec(memory_space=pl.ANY)
DP, COUNT, OWNERS = range(3)


def later(values, *before):
    return lax.optimization_barrier((values, before))[0]


def sibling(value):
    return lax.ppermute(value, "dp", [(d, d ^ 1) for d in range(lax.axis_size("dp"))])


def shifted(value, steps):
    count = lax.axis_size("dp")
    return lax.ppermute(value, "dp", [(d, (d + 2 * steps) % count) for d in range(count)])


def moved_rows(local):
    depth = lax.axis_size("dp") // 2
    return [local] + [shifted(local, k) for k in range(1, depth)]


def moved_passed(down, up=None):
    sections = lax.axis_size("section")
    count = lax.axis_size("dp")

    def moved(local, direction, k):
        pairs = [
            (s * count + d, (s + direction) % sections * count + (d + 2 * k) % count)
            for s in range(sections)
            for d in range(count)
        ]
        return lax.ppermute(local, ("section", "dp"), pairs)

    both = down[None] if up is None else jnp.stack([down, up])
    if sections == 2:
        return [moved(both, 1, k) for k in range(count // 2)]
    return [jnp.stack([moved(down, -1, k), moved(up, 1, k)]) for k in range(count // 2)]


def halves(pieces):
    mine = [jnp.concatenate([piece[i] for piece in pieces]) for i in range(pieces[0].shape[0])]
    return [[half, sibling(half)] for half in mine]


def scatter_pairs(kept, sent):
    return summed_pairs(kept, sibling(sent))


def summed_pairs(kept, got):
    depth = lax.axis_size("dp") // 2
    return (kept + got.astype(F32)).reshape((depth, kept.shape[0] // depth, kept.shape[1]))


def scatter_parts(pairs):
    return [pairs[0]] + [shifted(pairs[k].astype(BF16), -k) for k in range(1, pairs.shape[0])]


def added(rows, parts):
    return sum([part.astype(F32) for part in parts], rows.astype(F32)).astype(BF16)


def tensor_parts(value):
    count = lax.axis_size("tensor")
    step = 1
    while True:
        got = lax.ppermute(value, "tensor", [(t, t ^ step) for t in range(count)])
        step *= 2
        if step >= count:
            return value, got
        value = value + got


def tile_of(size):
    return 256 if size % 256 == 0 else BLK


def call(kernel, name, outs, operands, specs, flops, moved, scratch=()):
    return pl.pallas_call(
        kernel,
        out_shape=outs,
        in_specs=specs,
        out_specs=[VMEM] * len(outs),
        scratch_shapes=scratch,
        compiler_params=pltpu.CompilerParams(vmem_limit_bytes=12 * MIB),
        cost_estimate=pl.CostEstimate(flops=1, bytes_accessed=1, transcendentals=0),
        name=name,
    )(*operands)


def struct(*shape, dtype=BF16):
    return jax.ShapeDtypeStruct(shape, dtype)


def nt_dot(left, right):
    return lax.dot_general(left, right, (((1,), (1,)), ((), ())), preferred_element_type=F32)


def load_kernel(up_in, down_in, after, up, down, sems):
    copies = [pltpu.make_async_copy(up_in, up, sems.at[0]), pltpu.make_async_copy(down_in, down, sems.at[1])]
    for copy in copies:
        copy.start()
    for copy in copies:
        copy.wait()


def load_one_kernel(source, *refs):
    target, sem = refs[-2:]
    copy = pltpu.make_async_copy(source, target, sem)
    copy.start()
    copy.wait()


def load_one(weight, after):
    return pl.pallas_call(
        load_one_kernel,
        out_shape=pltpu.VMEM(weight.shape, BF16),
        in_specs=[HBM] + [ANY] * len(after),
        out_specs=VMEM,
        scratch_shapes=[pltpu.SemaphoreType.DMA(())],
        compiler_params=pltpu.CompilerParams(vmem_limit_bytes=8 * MIB),
        name="load_weight",
    )(in_hbm(weight), *after)


def first_kernel(flag, stash, begin, start, out, sems):
    stashed = pltpu.make_async_copy(stash.at[flag[0]], out.at[0], sems.at[0])
    stashed.start()

    @pl.when(flag[0] == 1)
    def _():
        copy = pltpu.make_async_copy(begin, out.at[1], sems.at[1])
        copy.start()
        copy.wait()

    @pl.when(flag[0] == 0)
    def _():
        copy = pltpu.make_async_copy(start, out.at[1], sems.at[1])
        copy.start()
        copy.wait()

    stashed.wait()


def first_rows_of(flag, stash, begin, start):
    return pl.pallas_call(
        first_kernel,
        out_shape=struct(2, *begin.shape),
        in_specs=[SMEM] + [HBM] * 3,
        out_specs=VMEM,
        scratch_shapes=[pltpu.SemaphoreType.DMA((2,))],
        compiler_params=pltpu.CompilerParams(vmem_limit_bytes=2 * MIB),
        name="first_rows",
    )(flag, *map(in_hbm, [stash, begin, start]))


def load_weights(up, down, after):
    return pl.pallas_call(
        load_kernel,
        out_shape=[pltpu.VMEM(up.shape, BF16), pltpu.VMEM(down.shape, BF16)],
        in_specs=[HBM] * 2 + [ANY],
        out_specs=[VMEM] * 2,
        scratch_shapes=[pltpu.SemaphoreType.DMA((2,))],
        compiler_params=pltpu.CompilerParams(vmem_limit_bytes=16 * MIB),
        name="load_weights",
    )(in_hbm(up), in_hbm(down), after)


def in_hbm(value):
    return pltpu.with_memory_space_constraint(value, pltpu.HBM)


def write_products(rows, gain, up, sent, normed):
    widened = rows.astype(F32)
    squares = jnp.sum(widened * widened, axis=1, keepdims=True)
    normed[...] = (widened * gain[...].astype(F32)).astype(BF16)
    hidden = up.shape[1]
    step = tile_of(hidden)
    for n in range(0, hidden, step):
        sent[:, n : n + step] = jnp.dot(normed[...], up[:, n : n + step], preferred_element_type=F32).astype(BF16)
    coarse = squares.astype(BF16).astype(F32)
    lane = lax.broadcasted_iota(jnp.int32, (rows.shape[0], BLK), 1)
    sent[:, hidden:] = jnp.where(lane == 0, coarse, jnp.where(lane == 1, squares - coarse, 0.0)).astype(BF16)


def write_act_grads(grads, down, sent):
    hidden = down.shape[0]
    step = tile_of(hidden)
    for n in range(0, hidden, step):
        sent[:, n : n + step] = nt_dot(grads[...], down[n : n + step, :]).astype(BF16)


def joined(low, high):
    return jnp.concatenate([low[...], high[...]], axis=0)


def product_kernel(low, high, gain, up, *refs):
    sent, normed = refs[-2:]
    write_products(joined(low, high), gain, up, sent, normed)


def products(row_halves, gain, up, down):
    rows = 2 * row_halves[0].shape[0]
    channels, hidden = up.shape
    operands = [*row_halves, gain, up, *down]
    return call(
        product_kernel, "products", [struct(rows, hidden + BLK)],
        operands, [VMEM] * len(operands), 2 * rows * channels * hidden, 2 * channels * hidden,
        [pltpu.VMEM((rows, channels), BF16)],
    )[0]


def act_kernel(low, high, down, _, sent, grads):
    grads[...] = joined(low, high)
    write_act_grads(grads, down, sent)


def act_grads(grad_halves, up, down):
    rows = 2 * grad_halves[0].shape[0]
    hidden, channels = down.shape
    return call(
        act_kernel, "act_grads", [struct(rows, hidden)],
        [*grad_halves, down, up], [VMEM] * 4, 2 * rows * channels * hidden, 2 * channels * hidden,
        [pltpu.VMEM((rows, channels), BF16)],
    )[0]


def product_act_kernel(low, high, grad_low, grad_high, gain, up, down, sent, normed):
    width = up.shape[1] + BLK
    write_products(joined(low, high), gain, up, sent.at[:, :width], normed)
    normed[...] = joined(grad_low, grad_high)
    write_act_grads(normed, down, sent.at[:, width:])


def products_and_act_grads(row_halves, grad_halves, gain, up, down):
    rows = 2 * row_halves[0].shape[0]
    channels, hidden = up.shape
    return call(
        product_act_kernel, "products_and_act_grads", [struct(rows, 2 * hidden + BLK)],
        [*row_halves, *grad_halves, gain, up, down], [VMEM] * 7, 4 * rows * channels * hidden, 4 * channels * hidden,
        [pltpu.VMEM((rows, channels), BF16)],
    )[0]


def scales_in(own, got, hidden, width):
    tail = own[:, hidden:].astype(F32) + got[:, hidden:].astype(F32)
    return lax.rsqrt((tail[:, 0:1] + tail[:, 1:2]) / width + EPSILON)


def gate_of(hidden):
    return 1.0 / (1.0 + jnp.exp(-hidden))


def write_backward(width, own, got, act_own, act_got, low, high, gain, up, kept, sent, scaled, activated):
    channels, hidden = up.shape
    scales = scales_in(own, got, hidden, width)
    scale_grad = jnp.zeros_like(scales)
    step = tile_of(hidden)
    for n in range(0, hidden, step):
        cut = slice(n, n + step)
        product = own[:, cut].astype(F32) + got[:, cut].astype(F32)
        act_grad = act_own[:, cut].astype(F32) + act_got[:, cut].astype(F32)
        value = product * scales
        gate = gate_of(value)
        activated[:, cut] = (value * gate).astype(BF16)
        grad = act_grad * gate * (1.0 + value * (1.0 - gate))
        scaled[:, cut] = (grad * scales).astype(BF16)
        scale_grad += jnp.sum(grad * product, axis=1, keepdims=True)
    factor = scale_grad * scales * scales * scales / width
    half = low.shape[0]
    step = tile_of(channels)
    for c in range(0, channels, step):
        cut = slice(c, c + step)
        part = nt_dot(scaled[...], up[cut, :]) * gain[:, cut].astype(F32)
        kept[:, cut] = part[:half] - factor[:half] * low[:, cut].astype(F32)
        sent[:, cut] = (part[half:] - factor[half:] * high[:, cut].astype(F32)).astype(BF16)


def write_forward(width, own, got, down, kept, sent, activated):
    hidden, channels = down.shape
    scales = scales_in(own, got, hidden, width)
    step = tile_of(hidden)
    for n in range(0, hidden, step):
        cut = slice(n, n + step)
        value = (own[:, cut].astype(F32) + got[:, cut].astype(F32)) * scales
        activated[:, cut] = (value * gate_of(value)).astype(BF16)
    half = kept.shape[0]
    step = tile_of(channels)
    for c in range(0, channels, step):
        cut = slice(c, c + step)
        part = jnp.dot(activated[...], down[:, cut], preferred_element_type=F32)
        kept[:, cut] = part[:half]
        sent[:, cut] = part[half:].astype(BF16)


def backward_kernel(width, own, got, act_own, act_got, low, high, gain, up, _, *refs):
    write_backward(width, own, got, act_own, act_got, low, high, gain, up, *refs[-4:])


def joint_backward_kernel(width, own, got, low, high, gain, up, _, *refs):
    cut = up.shape[1] + BLK
    write_backward(
        width, own.at[:, :cut], got.at[:, :cut], own.at[:, cut:], got.at[:, cut:], low, high, gain, up, *refs[-4:]
    )


def joint_backward(width, parts, row_halves, gain, up, down, after):
    half, channels = row_halves[0].shape
    hidden = up.shape[1]
    outs = [struct(half, channels, dtype=F32), struct(half, channels), struct(2 * half, hidden), struct(2 * half, hidden)]
    operands = [*parts, *row_halves, gain, up, down]
    return call(
        functools.partial(joint_backward_kernel, width), "backward", outs, operands + after,
        [VMEM] * len(operands) + [ANY] * len(after),
        4 * half * channels * hidden, 2 * channels * hidden,
    )


def backward(width, products_parts, act_parts, row_halves, gain, up, down, after):
    half, channels = row_halves[0].shape
    hidden = up.shape[1]
    outs = [struct(half, channels, dtype=F32), struct(half, channels), struct(2 * half, hidden), struct(2 * half, hidden)]
    operands = [*products_parts, *act_parts, *row_halves, gain, up, down]
    return call(
        functools.partial(backward_kernel, width), "backward", outs, operands + after,
        [VMEM] * len(operands) + [ANY] * len(after),
        4 * half * channels * hidden, 2 * channels * hidden,
    )


def forward_kernel(width, own, got, down, _, *refs):
    write_forward(width, own, got, down, *refs[-3:])


def forward(width, products_parts, up, down, after):
    rows = products_parts[0].shape[0]
    hidden, channels = down.shape
    outs = [struct(rows // 2, channels, dtype=F32), struct(rows // 2, channels)]
    return call(
        functools.partial(forward_kernel, width), "forward", outs, [*products_parts, down, up, *after],
        [VMEM] * 4 + [ANY] * len(after),
        2 * rows * channels * hidden, 2 * channels * hidden, [pltpu.VMEM((rows, hidden), BF16)],
    )


def enter_kernel(forward_in, flag, low, high, other_low, other_high, gain, up, down, sent, grads, normed):
    @pl.when(flag[0] == forward_in)
    def _():
        write_products(joined(low, high), gain, up, sent, normed)
        grads[...] = joined(other_low, other_high)

    @pl.when(flag[0] != forward_in)
    def _():
        grads[...] = joined(low, high)
        write_act_grads(grads, down, sent)
        sent[:, up.shape[1] :] = jnp.zeros((sent.shape[0], BLK), BF16)


def enter(forward_in, flag, row_halves, other_halves, gain, up, down):
    rows = 2 * row_halves[0].shape[0]
    channels, hidden = up.shape
    return call(
        functools.partial(enter_kernel, forward_in), "enter", [struct(rows, hidden + BLK), struct(rows, channels)],
        [flag, *row_halves, *other_halves, gain, up, down], [SMEM] + [VMEM] * 7,
        2 * rows * channels * hidden, 2 * channels * hidden, [pltpu.VMEM((rows, channels), BF16)],
    )


def leave_kernel(forward_in, width, flag, own, got, back_own, back_got, low, high, gain, up, down, *refs):
    kept, sent, scaled, activated, scratch = refs[-5:]

    @pl.when(flag[0] == forward_in)
    def _():
        write_forward(width, own, got, down, kept, sent, scratch)

    @pl.when(flag[0] != forward_in)
    def _():
        write_backward(width, back_own, back_got, own, got, low, high, gain, up, kept, sent, scaled, activated)


def leave(width, forward_in, flag, parts, back_parts, row_halves, gain, up, down, filled, after):
    half, channels = row_halves[0].shape
    hidden = up.shape[1]
    outs = [struct(half, channels, dtype=F32), struct(half, channels), struct(2 * half, hidden), struct(2 * half, hidden)]
    operands = [flag, *parts, *back_parts, *row_halves, gain, up, down, *filled]
    first = len(operands) - len(filled)
    return pl.pallas_call(
        functools.partial(leave_kernel, forward_in, width),
        out_shape=outs,
        in_specs=[SMEM] + [VMEM] * (len(operands) - 1) + [ANY] * len(after),
        out_specs=[VMEM] * 4,
        scratch_shapes=[pltpu.VMEM((2 * half, hidden), BF16)],
        input_output_aliases={first + i: 2 + i for i in range(len(filled))},
        compiler_params=pltpu.CompilerParams(vmem_limit_bytes=12 * MIB),
        cost_estimate=pl.CostEstimate(flops=1, bytes_accessed=1, transcendentals=0),
        name="leave",
    )(*operands, *after)


def block_kernel(channel_blocks, hidden_blocks, depth, capacity, table_counts, plan, gain, *refs):
    *tables, out = refs
    up_count = channel_blocks * hidden_blocks
    dp_index = plan[0, DP]
    z, core = dp_index // 2, lax.rem(dp_index, 2)

    def per_slot(slot, carry):
        owner = 2 * lax.rem(z - lax.rem(slot, depth) + depth, depth) + lax.rem(core + slot // depth, 2)
        number = jnp.int32(-1)
        for entry in range(capacity):
            here = jnp.logical_and(plan[dp_index, OWNERS + entry] == owner, entry < plan[dp_index, COUNT])
            number = jnp.where(here, plan[dp_index, OWNERS + capacity + entry], number)
        is_up = number < up_count
        down_number = jnp.maximum(number - up_count, 0)
        up_number = jnp.maximum(number, 0)
        left_index = jnp.where(is_up, up_number // hidden_blocks, down_number // channel_blocks)
        right_index = jnp.where(is_up, lax.rem(up_number, hidden_blocks), lax.rem(down_number, channel_blocks))
        left = pl.ds(pl.multiple_of(left_index * BLK, BLK), BLK)
        right = pl.ds(pl.multiple_of(right_index * BLK, BLK), BLK)

        def both(halves, cut):
            return jnp.concatenate([half[:, cut] for half in halves], axis=0)

        groups = []
        start = 0
        for count in table_counts:
            groups.append(tables[start : start + count])
            start += count

        def write(is_up_block):
            total = jnp.zeros((BLK, BLK), F32)
            for group in groups:
                rows, scaled, activated, grads = group[:2], group[2], group[3], group[4:]
                if is_up_block:
                    first = (both(rows, left).astype(F32) * gain[:, left].astype(F32)).astype(BF16)
                    second = scaled[:, right]
                else:
                    first = activated[:, left]
                    second = both(grads, right)
                total += lax.dot_general(first, second, (((0,), (0,)), ((), ())), preferred_element_type=F32)
            out[slot] = total.astype(BF16)

        @pl.when(jnp.logical_and(number >= 0, is_up))
        def _():
            write(True)

        @pl.when(jnp.logical_not(is_up))
        def _():
            write(False)

        @pl.when(number < 0)
        def _():
            out[slot] = jnp.zeros((BLK, BLK), BF16)

        return carry

    lax.fori_loop(0, out.shape[0], per_slot, 0)


def outgoing_blocks(plan, capacity, gain, tables, channel_blocks, hidden_blocks):
    slots = lax.axis_size("dp")
    flat = [table for turn in tables for table in turn]
    kernel = functools.partial(
        block_kernel, channel_blocks, hidden_blocks, slots // 2, capacity, [len(turn) for turn in tables]
    )
    return call(
        kernel, "block_grads", [struct(slots, BLK, BLK)], [plan, gain, *flat],
        [SMEM, VMEM] + [VMEM] * len(flat), 4 * slots * BLK * BLK * BLK, 2 * slots * BLK * BLK,
    )[0]


def adam_kernel(depth, plan, relayed, *refs):
    others = refs[: depth - 1]
    first, second, *rest = refs[depth - 1 :]
    outs, (first_new, second_new, direction), sems = rest[-7:-4], rest[-4:-1], rest[-1]
    dp_index = plan[0, DP]
    z, core = dp_index // 2, lax.rem(dp_index, 2)
    slots, capacity = plan.shape[0], first.shape[0]

    def copies(place):
        return [
            pltpu.make_async_copy(new.at[place], out.at[place], sems.at[i, place])
            for i, (new, out) in enumerate(zip((first_new, second_new, direction), outs))
        ]

    def update(place, grad):
        grad = grad.astype(F32)
        first_next = 0.9 * first[place] + 0.1 * grad
        second_next = 0.999 * second[place] + 0.001 * grad * grad
        first_new[place] = first_next
        second_new[place] = second_next
        direction[place] = first_next / (jnp.sqrt(second_next) + 1e-08)
        for copy in copies(place):
            copy.start()

    def per_source(source, place):
        sends = False
        for entry in range(capacity):
            sends = jnp.logical_or(sends, jnp.logical_and(plan[source, OWNERS + entry] == dp_index, entry < plan[source, COUNT]))
        back = lax.rem(source // 2 - z + depth, depth)
        across = lax.rem(source + core, 2)
        for k in range(depth):
            @pl.when(jnp.logical_and(sends, back == k))
            def _():
                if k == 0:
                    update(place, relayed[0])
                else:
                    update(place, others[k - 1][pl.ds(pl.multiple_of(across * BLK, BLK), BLK)])

        return place + jnp.where(sends, 1, 0)

    count = lax.fori_loop(0, slots, per_source, 0)

    def empty(place, carry):
        for new in (first_new, second_new, direction):
            new[place] = jnp.zeros((BLK, BLK), F32)
        for copy in copies(place):
            copy.start()
        return carry

    lax.fori_loop(count, capacity, empty, 0)
    for place in range(capacity):
        for copy in copies(place):
            copy.wait()


def adam(plan, relayed, others, first, second, after):
    shape = jax.ShapeDtypeStruct(first.shape, F32)
    operands = [plan, relayed, *others, first, second]
    return pl.pallas_call(
        functools.partial(adam_kernel, lax.axis_size("dp") // 2),
        out_shape=[shape] * 3,
        in_specs=[SMEM] + [VMEM] * (len(operands) - 1) + [ANY] * len(after),
        out_specs=[HBM] * 3,
        scratch_shapes=[pltpu.VMEM(first.shape, F32)] * 3 + [pltpu.SemaphoreType.DMA((3, first.shape[0]))],
        compiler_params=pltpu.CompilerParams(vmem_limit_bytes=12 * MIB),
        name="adam_step",
    )(*operands, *after)


def finish_kernel(earlier_count, *refs):
    earlier, rows, parts, out = refs[:earlier_count], refs[earlier_count], refs[earlier_count + 1 : -1], refs[-1]
    for turn in range(earlier_count):
        out[turn] = earlier[turn][...]
    total = rows[...].astype(F32)
    for part in parts:
        total += part[...].astype(F32)
    out[earlier_count] = total.astype(BF16)


def finish(earlier, rows, parts):
    operands = [*earlier, rows, *parts]
    return call(
        functools.partial(finish_kernel, len(earlier)), "finish", [struct(len(earlier) + 1, *rows.shape)], operands,
        [VMEM] * len(operands), rows.size, 8 * rows.size,
    )[0]


def finish_pair_kernel(depth, flag, chained, off_grads, off_rows, chain_rows, *refs):
    off_parts, chain_parts, (section_out, grads_out, done) = refs[:depth], refs[depth : 2 * depth], refs[2 * depth :]
    done[...] = jnp.zeros(done.shape, F32)

    def total(local, parts):
        value = local[...].astype(F32)
        for part in parts:
            value += part[...].astype(F32)
        return value.astype(BF16)

    off_back = total(off_grads, [part.at[0] for part in off_parts])
    off_forward = total(off_rows, [part.at[1] for part in off_parts])
    later_turn = total(chain_rows, chain_parts)

    @pl.when(flag[0] == 1)
    def _():
        section_out[0] = chained[...]
        section_out[1] = off_forward
        grads_out[0] = off_back
        grads_out[1] = later_turn

    @pl.when(flag[0] == 0)
    def _():
        section_out[0] = off_forward
        section_out[1] = later_turn
        grads_out[0] = chained[...]
        grads_out[1] = off_back


def finish_pair(flag, chained, off_grads, off_rows, chain_rows, off_parts, chain_parts):
    operands = [flag, chained, off_grads, off_rows, chain_rows, *off_parts, *chain_parts]
    return call(
        functools.partial(finish_pair_kernel, len(off_parts)), "finish_pair",
        [struct(2, *chained.shape)] * 2 + [struct(8, BLK, dtype=F32)], operands,
        [SMEM] + [VMEM] * (len(operands) - 1), 8 * chained.size, 16 * chained.size,
    )


def relay_pair(
    live_rows, arriving, entering, begin, start, stash, gain, up, down, width, plan, exchange
):
    rows = begin.shape[0]
    is_first = lax.axis_index("section") == 0
    flag = is_first.astype(jnp.int32).reshape(1)
    first = first_rows_of(flag, stash, begin, start)
    row_start = lax.axis_index("dp") * rows
    up, down, is_first, row_start, plan = lax.optimization_barrier((up, down, is_first, row_start, plan))

    with jax.named_scope("gather_first"):
        moved = moved_rows(first)
    up = load_one(up, [first, plan])
    with jax.named_scope("gather_first"):
        back_halves, chain_halves = halves(later(moved, up))
    back_product = products(back_halves, gain, up, [])
    down = load_one(down, [back_product])
    with jax.named_scope("swap_back"):
        back_parts = tensor_parts(back_product)
    entered, _ = enter(1, flag, later(chain_halves, back_product), chain_halves, gain, up, down)
    with jax.named_scope("swap_chain0"):
        parts = tensor_parts(entered)
    live = (row_start + lax.iota(jnp.int32, rows) < live_rows[0])[:, None]

    def pick(in_first, in_last):
        return jnp.where(is_first, in_first, in_last)

    others = jnp.stack([
        pick(stash[0], stash[1]),
        pick(start, jnp.where(live, later(arriving, entered)[0], jnp.zeros((), BF16))),
        pick(later(entering, entered)[0], begin),
    ])
    off_grads, off_rows = others[1], others[2]
    with jax.named_scope("gather_others"):
        off_halves, off_grad_halves, off_row_halves = halves(later(moved_rows(later(others, entered)), back_parts[1]))
    off_product = products_and_act_grads(off_halves, off_grad_halves, gain, up, down)
    with jax.named_scope("swap_off_back"):
        off_parts = tensor_parts(off_product)
    off_forward = products(later(off_row_halves, off_product), gain, up, [down])
    with jax.named_scope("swap_off_forward"):
        off_forward_parts = tensor_parts(off_forward)

    with jax.named_scope("chain0"):
        kept, sent, scaled, activated = leave(
            width, 1, flag, parts, back_parts, back_halves, gain, up, down, [], [off_product, off_forward]
        )
        chained = added(first[1], scatter_parts(scatter_pairs(kept, sent)))
    with jax.named_scope("off_back"):
        kept, sent, off_scaled, off_activated = joint_backward(width, off_parts, off_halves, gain, up, down, [])
        off_back_pairs = scatter_pairs(kept, sent)
    with jax.named_scope("pass"):
        passed = later(halves(moved_passed(chained))[0], kept)
    chain_in = passed[0][:rows]
    entered, grads = enter(0, flag, passed, chain_halves, gain, up, down)
    with jax.named_scope("swap_chain1"):
        parts = tensor_parts(entered)
    with jax.named_scope("off_forward"):
        kept, sent = forward(width, off_forward_parts, up, down, [entered])
        pairs = jnp.stack([off_back_pairs, scatter_pairs(kept, sent)], axis=1)
        off_sums = scatter_parts(pairs)
    with jax.named_scope("chain1"):
        kept, sent, scaled, activated = leave(
            width, 0, flag, parts, back_parts, back_halves, gain, up, down, [scaled, activated], [pairs]
        )
        got = sibling(sent)
        chain_sums = scatter_parts(summed_pairs(kept, got))
        off_sums = later(off_sums, kept)
    tables = [
        (*back_halves, scaled, activated, grads),
        (*off_halves, off_scaled, off_activated, *off_grad_halves),
    ]
    relayed, from_others = exchange(later(plan, off_sums), tables, got)
    section_outputs, input_grads, done = finish_pair(
        flag, chained, off_grads, off_rows, chain_in, off_sums, chain_sums
    )
    return section_outputs, input_grads, plan, relayed, from_others, [done]


def relay(
    is_first, is_last, masked, entering, section_inputs, grad_outputs, stashed_inputs, gain, up, down, width
):
    turn_count = stashed_inputs.shape[1]
    local_rows = section_inputs.shape[1]
    up, down, is_first, is_last, masked = lax.optimization_barrier((up, down, is_first, is_last, masked))
    grads_in, rows_in = grad_outputs[0], section_inputs[0]
    first = jnp.concatenate([stashed_inputs[0, :1], grad_outputs])
    with jax.named_scope("gather_first"):
        moved = moved_rows(first)
    up, down = load_weights(up, down, first)
    with jax.named_scope("gather_first"):
        gathered = halves(later(moved, up))
    stash_rows = [gathered[0]]
    grad_halves = gathered[1]
    back_products = [products(stash_rows[0], gain, up, [down])]
    with jax.named_scope("swap_b0p"):
        back_parts = [tensor_parts(back_products[0])]
    act_grad = act_grads(later(grad_halves, back_products[0]), up, down)
    with jax.named_scope("swap_b0a"):
        act_parts = tensor_parts(act_grad)
    with jax.named_scope("gather_others"):
        others = jnp.concatenate([section_inputs, stashed_inputs[0, 1:]])
        gathered = halves(moved_rows(later(others, act_grad)))
    product = products(gathered[0], gain, up, [down])
    with jax.named_scope("swap_f0p"):
        parts = tensor_parts(product)
    ahead = [product]
    for turn in range(1, turn_count):
        stash_rows.append(gathered[turn])
        back_products.append(products(stash_rows[turn], gain, up, [down]))
        ahead.append(back_products[turn])
        with jax.named_scope("swap_b1p"):
            back_parts.append(tensor_parts(back_products[turn]))

    forward_results = []
    backward_results = []
    tables = []
    for turn in range(turn_count):
        with jax.named_scope(f"backward{turn}"):
            kept, sent, scaled, activated = backward(
                width, back_parts[turn], act_parts, stash_rows[turn], gain, up, down, ahead
            )
            back_pairs = scatter_pairs(kept, sent)
        tables.append((*stash_rows[turn], scaled, activated, *grad_halves))
        if turn + 1 == turn_count:
            with jax.named_scope(f"backward{turn}"):
                back_sums = scatter_parts(back_pairs)
            parts = later(parts, back_sums)
        with jax.named_scope(f"forward{turn}"):
            kept, sent = forward(width, parts, up, down, [])
            pairs = scatter_pairs(kept, sent)
        if turn + 1 == turn_count:
            with jax.named_scope(f"forward{turn}"):
                sums = scatter_parts(pairs)
            input_grads = finish(backward_results, grads_in, back_sums)
            section_outputs = finish(forward_results, rows_in, sums)
            break
        with jax.named_scope(f"scatter{turn}"):
            sums = scatter_parts(jnp.stack([back_pairs, pairs], axis=1))
        backward_results.append(added(grads_in, [part[0] for part in sums]))
        forward_results.append(added(rows_in, [part[1] for part in sums]))
        with jax.named_scope(f"gather{turn}"):
            moved = moved_passed(
                jnp.where(is_first, masked[turn], backward_results[-1]),
                jnp.where(is_last, entering[turn], forward_results[-1]),
            )
            passed = halves(later(moved, back_parts[turn + 1][1]))
        grad_halves = passed[0]
        grads_in, rows_in = passed[0][0][:local_rows], passed[1][0][:local_rows]
        act_grad = act_grads(grad_halves, up, down)
        with jax.named_scope("swap_b1a"):
            act_parts = tensor_parts(act_grad)
        product = products(later(passed[1], act_grad), gain, up, [down])
        with jax.named_scope("swap_f1p"):
            parts = tensor_parts(product)
        ahead = []
    return section_outputs, input_grads, tables


def body(
    section_inputs,
    entering,
    grad_outputs,
    arriving,
    live_rows,
    stashed_inputs,
    norm_gain,
    up_weight,
    down_weight,
    held_blocks,
    held_count,
    held_owner,
    first_moment,
    second_moment,
):
    section_count = lax.axis_size("section")
    section_index = lax.axis_index("section")
    dp_count = lax.axis_size("dp")
    turn_count = stashed_inputs.shape[1]
    local_rows = section_inputs.shape[1]
    channels, hidden = up_weight.shape[1:]
    width = channels * lax.axis_size("tensor")
    is_first = section_index == 0
    is_last = section_index == section_count - 1
    counts, owners, blocks = held_count[0, 0], held_owner[0, 0], held_blocks[0, 0]
    capacity = owners.shape[1]
    dp_index = lax.axis_index("dp")
    plan = jnp.concatenate([jnp.full((dp_count, 1), dp_index, jnp.int32), counts[:, None], owners, blocks], axis=1)

    def exchange(plan, tables, before):
        with jax.named_scope("block_exchange"):
            outgoing = outgoing_blocks(plan, capacity, norm_gain, tables, channels // BLK, hidden // BLK)
            outgoing = outgoing.reshape((2, dp_count // 2, BLK, BLK))
            relayed = later(sibling(outgoing[1]), before)
            pairs = [jnp.concatenate([outgoing[0, k], relayed[k]]) for k in range(1, dp_count // 2)]
            return relayed, [shifted(pair, -k - 1) for k, pair in enumerate(pairs)]

    if section_count == 2 and turn_count == 2:
        section_outputs, input_grads, plan, relayed, others, after = relay_pair(
            live_rows, arriving, entering, section_inputs[0], grad_outputs[0], stashed_inputs[0], norm_gain,
            up_weight[0], down_weight[0], width, plan, exchange,
        )
    else:
        row_ids = dp_index * local_rows + lax.iota(jnp.int32, local_rows)
        masked = jnp.where((row_ids < live_rows[:, None])[..., None], arriving, jnp.zeros((), BF16))
        section_outputs, input_grads, tables = relay(
            is_first, is_last, masked, entering, section_inputs, grad_outputs, stashed_inputs, norm_gain,
            up_weight[0], down_weight[0], width,
        )
        relayed, others = exchange(plan, tables, None)
        after = []
    first_out, second_out, direction_out = adam(
        plan, relayed, others, first_moment[0, 0, 0], second_moment[0, 0, 0], after
    )
    return (
        section_outputs[None],
        input_grads[None],
        first_out[None, None, None],
        second_out[None, None, None],
        direction_out[None, None, None],
    )


def solution(mesh):
    return jax.shard_map(
        body,
        mesh=mesh,
        in_specs=(
            P("section", "dp", "tensor"),
            P(None, "dp", "tensor"),
            P("section", "dp", "tensor"),
            P(None, "dp", "tensor"),
            P(),
            P("section", None, "dp", "tensor"),
            P("section", "tensor"),
            P("section", "tensor", "dp"),
            P("section", "dp", "tensor"),
            P("section", "tensor", None, None),
            P("section", "tensor", None),
            P("section", "tensor", None, None),
            P("section", "tensor", "dp", None, None, None),
            P("section", "tensor", "dp", None, None, None),
        ),
        out_specs=(
            P("section", None, "dp", "tensor"),
            P("section", None, "dp", "tensor"),
            P("section", "tensor", "dp", None, None, None),
            P("section", "tensor", "dp", None, None, None),
            P("section", "tensor", "dp", None, None, None),
        ),
        check_vma=False,
    )
```

```python
import functools

import jax
import jax.numpy as jnp
from jax import lax
from jax.experimental import pallas as pl
from jax.experimental.pallas import tpu as pltpu
from jax.sharding import PartitionSpec as P

BLK = 128
EPSILON = 1e-06
BF16 = jnp.bfloat16
F32 = jnp.float32
MIB = 1024 * 1024
VMEM = pl.BlockSpec(memory_space=pltpu.VMEM)
SMEM = pl.BlockSpec(memory_space=pltpu.SMEM)
HBM = pl.BlockSpec(memory_space=pltpu.HBM)
ANY = pl.BlockSpec(memory_space=pl.ANY)
DP, COUNT, OWNERS = range(3)


def later(values, *before):
    return lax.optimization_barrier((values, before))[0]


def sibling(value):
    return lax.ppermute(value, "dp", [(d, d ^ 1) for d in range(lax.axis_size("dp"))])


def shifted(value, steps):
    count = lax.axis_size("dp")
    return lax.ppermute(value, "dp", [(d, (d + 2 * steps) % count) for d in range(count)])


def moved_rows(local):
    depth = lax.axis_size("dp") // 2
    return [local] + [shifted(local, k) for k in range(1, depth)]


def moved_passed(down, up=None):
    sections = lax.axis_size("section")
    count = lax.axis_size("dp")

    def moved(local, direction, k):
        pairs = [
            (s * count + d, (s + direction) % sections * count + (d + 2 * k) % count)
            for s in range(sections)
            for d in range(count)
        ]
        return lax.ppermute(local, ("section", "dp"), pairs)

    both = down[None] if up is None else jnp.stack([down, up])
    if sections == 2:
        return [moved(both, 1, k) for k in range(count // 2)]
    return [jnp.stack([moved(down, -1, k), moved(up, 1, k)]) for k in range(count // 2)]


def halves(pieces):
    mine = [jnp.concatenate([piece[i] for piece in pieces]) for i in range(pieces[0].shape[0])]
    return [[half, sibling(half)] for half in mine]


def scatter_pairs(kept, sent):
    return summed_pairs(kept, sibling(sent))


def summed_pairs(kept, got):
    depth = lax.axis_size("dp") // 2
    return (kept + got.astype(F32)).reshape((depth, kept.shape[0] // depth, kept.shape[1]))


def scatter_parts(pairs):
    return [pairs[0]] + [shifted(pairs[k].astype(BF16), -k) for k in range(1, pairs.shape[0])]


def added(rows, parts):
    return sum([part.astype(F32) for part in parts], rows.astype(F32)).astype(BF16)


def tensor_parts(value):
    count = lax.axis_size("tensor")
    step = 1
    while True:
        got = lax.ppermute(value, "tensor", [(t, t ^ step) for t in range(count)])
        step *= 2
        if step >= count:
            return value, got
        value = value + got


def tile_of(size):
    return 256 if size % 256 == 0 else BLK


def call(kernel, name, outs, operands, specs, flops, moved, scratch=()):
    return pl.pallas_call(
        kernel,
        out_shape=outs,
        in_specs=specs,
        out_specs=[VMEM] * len(outs),
        scratch_shapes=scratch,
        compiler_params=pltpu.CompilerParams(vmem_limit_bytes=12 * MIB),
        cost_estimate=pl.CostEstimate(flops=1, bytes_accessed=1, transcendentals=0),
        name=name,
    )(*operands)


def struct(*shape, dtype=BF16):
    return jax.ShapeDtypeStruct(shape, dtype)


def nt_dot(left, right):
    return lax.dot_general(left, right, (((1,), (1,)), ((), ())), preferred_element_type=F32)


def load_kernel(up_in, down_in, after, up, down, sems):
    copies = [pltpu.make_async_copy(up_in, up, sems.at[0]), pltpu.make_async_copy(down_in, down, sems.at[1])]
    for copy in copies:
        copy.start()
    for copy in copies:
        copy.wait()


def load_one_kernel(source, *refs):
    target, sem = refs[-2:]
    copy = pltpu.make_async_copy(source, target, sem)
    copy.start()
    copy.wait()


def load_one(weight, after):
    return pl.pallas_call(
        load_one_kernel,
        out_shape=pltpu.VMEM(weight.shape, BF16),
        in_specs=[HBM] + [ANY] * len(after),
        out_specs=VMEM,
        scratch_shapes=[pltpu.SemaphoreType.DMA(())],
        compiler_params=pltpu.CompilerParams(vmem_limit_bytes=8 * MIB),
        name="load_weight",
    )(in_hbm(weight), *after)


def first_kernel(flag, stash, begin, start, out, sems):
    stashed = pltpu.make_async_copy(stash.at[flag[0]], out.at[0], sems.at[0])
    stashed.start()

    @pl.when(flag[0] == 1)
    def _():
        copy = pltpu.make_async_copy(begin, out.at[1], sems.at[1])
        copy.start()
        copy.wait()

    @pl.when(flag[0] == 0)
    def _():
        copy = pltpu.make_async_copy(start, out.at[1], sems.at[1])
        copy.start()
        copy.wait()

    stashed.wait()


def first_rows_of(flag, stash, begin, start):
    return pl.pallas_call(
        first_kernel,
        out_shape=struct(2, *begin.shape),
        in_specs=[SMEM] + [HBM] * 3,
        out_specs=VMEM,
        scratch_shapes=[pltpu.SemaphoreType.DMA((2,))],
        compiler_params=pltpu.CompilerParams(vmem_limit_bytes=2 * MIB),
        name="first_rows",
    )(flag, *map(in_hbm, [stash, begin, start]))


def load_weights(up, down, after):
    return pl.pallas_call(
        load_kernel,
        out_shape=[pltpu.VMEM(up.shape, BF16), pltpu.VMEM(down.shape, BF16)],
        in_specs=[HBM] * 2 + [ANY],
        out_specs=[VMEM] * 2,
        scratch_shapes=[pltpu.SemaphoreType.DMA((2,))],
        compiler_params=pltpu.CompilerParams(vmem_limit_bytes=16 * MIB),
        name="load_weights",
    )(in_hbm(up), in_hbm(down), after)


def in_hbm(value):
    return pltpu.with_memory_space_constraint(value, pltpu.HBM)


def write_products(rows, gain, up, sent, normed):
    widened = rows.astype(F32)
    squares = jnp.sum(widened * widened, axis=1, keepdims=True)
    normed[...] = (widened * gain[...].astype(F32)).astype(BF16)
    hidden = up.shape[1]
    step = tile_of(hidden)
    for n in range(0, hidden, step):
        sent[:, n : n + step] = jnp.dot(normed[...], up[:, n : n + step], preferred_element_type=F32).astype(BF16)
    coarse = squares.astype(BF16).astype(F32)
    lane = lax.broadcasted_iota(jnp.int32, (rows.shape[0], BLK), 1)
    sent[:, hidden:] = jnp.where(lane == 0, coarse, jnp.where(lane == 1, squares - coarse, 0.0)).astype(BF16)


def write_act_grads(grads, down, sent):
    hidden = down.shape[0]
    step = tile_of(hidden)
    for n in range(0, hidden, step):
        sent[:, n : n + step] = nt_dot(grads[...], down[n : n + step, :]).astype(BF16)


def joined(low, high):
    return jnp.concatenate([low[...], high[...]], axis=0)


def product_kernel(low, high, gain, up, *refs):
    sent, normed = refs[-2:]
    write_products(joined(low, high), gain, up, sent, normed)


def products(row_halves, gain, up, down):
    rows = 2 * row_halves[0].shape[0]
    channels, hidden = up.shape
    operands = [*row_halves, gain, up, *down]
    return call(
        product_kernel, "products", [struct(rows, hidden + BLK)],
        operands, [VMEM] * len(operands), 2 * rows * channels * hidden, 2 * channels * hidden,
        [pltpu.VMEM((rows, channels), BF16)],
    )[0]


def act_kernel(low, high, down, _, sent, grads):
    grads[...] = joined(low, high)
    write_act_grads(grads, down, sent)


def act_grads(grad_halves, up, down):
    rows = 2 * grad_halves[0].shape[0]
    hidden, channels = down.shape
    return call(
        act_kernel, "act_grads", [struct(rows, hidden)],
        [*grad_halves, down, up], [VMEM] * 4, 2 * rows * channels * hidden, 2 * channels * hidden,
        [pltpu.VMEM((rows, channels), BF16)],
    )[0]


def product_act_kernel(low, high, grad_low, grad_high, gain, up, down, sent, normed):
    width = up.shape[1] + BLK
    write_products(joined(low, high), gain, up, sent.at[:, :width], normed)
    normed[...] = joined(grad_low, grad_high)
    write_act_grads(normed, down, sent.at[:, width:])


def products_and_act_grads(row_halves, grad_halves, gain, up, down):
    rows = 2 * row_halves[0].shape[0]
    channels, hidden = up.shape
    return call(
        product_act_kernel, "products_and_act_grads", [struct(rows, 2 * hidden + BLK)],
        [*row_halves, *grad_halves, gain, up, down], [VMEM] * 7, 4 * rows * channels * hidden, 4 * channels * hidden,
        [pltpu.VMEM((rows, channels), BF16)],
    )[0]


def scales_in(own, got, hidden, width):
    tail = own[:, hidden:].astype(F32) + got[:, hidden:].astype(F32)
    return lax.rsqrt((tail[:, 0:1] + tail[:, 1:2]) / width + EPSILON)


def gate_of(hidden):
    return 1.0 / (1.0 + jnp.exp(-hidden))


def write_backward(width, own, got, act_own, act_got, low, high, gain, up, kept, sent, scaled, activated):
    channels, hidden = up.shape
    scales = scales_in(own, got, hidden, width)
    scale_grad = jnp.zeros_like(scales)
    step = tile_of(hidden)
    for n in range(0, hidden, step):
        cut = slice(n, n + step)
        product = own[:, cut].astype(F32) + got[:, cut].astype(F32)
        act_grad = act_own[:, cut].astype(F32) + act_got[:, cut].astype(F32)
        value = product * scales
        gate = gate_of(value)
        activated[:, cut] = (value * gate).astype(BF16)
        grad = act_grad * gate * (1.0 + value * (1.0 - gate))
        scaled[:, cut] = (grad * scales).astype(BF16)
        scale_grad += jnp.sum(grad * product, axis=1, keepdims=True)
    factor = scale_grad * scales * scales * scales / width
    half = low.shape[0]
    step = tile_of(channels)
    for c in range(0, channels, step):
        cut = slice(c, c + step)
        part = nt_dot(scaled[...], up[cut, :]) * gain[:, cut].astype(F32)
        kept[:, cut] = part[:half] - factor[:half] * low[:, cut].astype(F32)
        sent[:, cut] = (part[half:] - factor[half:] * high[:, cut].astype(F32)).astype(BF16)


def write_forward(width, own, got, down, kept, sent, activated):
    hidden, channels = down.shape
    scales = scales_in(own, got, hidden, width)
    step = tile_of(hidden)
    for n in range(0, hidden, step):
        cut = slice(n, n + step)
        value = (own[:, cut].astype(F32) + got[:, cut].astype(F32)) * scales
        activated[:, cut] = (value * gate_of(value)).astype(BF16)
    half = kept.shape[0]
    step = tile_of(channels)
    for c in range(0, channels, step):
        cut = slice(c, c + step)
        part = jnp.dot(activated[...], down[:, cut], preferred_element_type=F32)
        kept[:, cut] = part[:half]
        sent[:, cut] = part[half:].astype(BF16)


def backward_kernel(width, own, got, act_own, act_got, low, high, gain, up, _, *refs):
    write_backward(width, own, got, act_own, act_got, low, high, gain, up, *refs[-4:])


def joint_backward_kernel(width, own, got, low, high, gain, up, _, *refs):
    cut = up.shape[1] + BLK
    write_backward(
        width, own.at[:, :cut], got.at[:, :cut], own.at[:, cut:], got.at[:, cut:], low, high, gain, up, *refs[-4:]
    )


def joint_backward(width, parts, row_halves, gain, up, down, after):
    half, channels = row_halves[0].shape
    hidden = up.shape[1]
    outs = [struct(half, channels, dtype=F32), struct(half, channels), struct(2 * half, hidden), struct(2 * half, hidden)]
    operands = [*parts, *row_halves, gain, up, down]
    return call(
        functools.partial(joint_backward_kernel, width), "backward", outs, operands + after,
        [VMEM] * len(operands) + [ANY] * len(after),
        4 * half * channels * hidden, 2 * channels * hidden,
    )


def backward(width, products_parts, act_parts, row_halves, gain, up, down, after):
    half, channels = row_halves[0].shape
    hidden = up.shape[1]
    outs = [struct(half, channels, dtype=F32), struct(half, channels), struct(2 * half, hidden), struct(2 * half, hidden)]
    operands = [*products_parts, *act_parts, *row_halves, gain, up, down]
    return call(
        functools.partial(backward_kernel, width), "backward", outs, operands + after,
        [VMEM] * len(operands) + [ANY] * len(after),
        4 * half * channels * hidden, 2 * channels * hidden,
    )


def forward_kernel(width, own, got, down, _, *refs):
    write_forward(width, own, got, down, *refs[-3:])


def forward(width, products_parts, up, down, after):
    rows = products_parts[0].shape[0]
    hidden, channels = down.shape
    outs = [struct(rows // 2, channels, dtype=F32), struct(rows // 2, channels)]
    return call(
        functools.partial(forward_kernel, width), "forward", outs, [*products_parts, down, up, *after],
        [VMEM] * 4 + [ANY] * len(after),
        2 * rows * channels * hidden, 2 * channels * hidden, [pltpu.VMEM((rows, hidden), BF16)],
    )


def enter_kernel(forward_in, flag, low, high, other_low, other_high, gain, up, down, sent, grads, normed):
    @pl.when(flag[0] == forward_in)
    def _():
        write_products(joined(low, high), gain, up, sent, normed)
        grads[...] = joined(other_low, other_high)

    @pl.when(flag[0] != forward_in)
    def _():
        grads[...] = joined(low, high)
        write_act_grads(grads, down, sent)
        sent[:, up.shape[1] :] = jnp.zeros((sent.shape[0], BLK), BF16)


def enter(forward_in, flag, row_halves, other_halves, gain, up, down):
    rows = 2 * row_halves[0].shape[0]
    channels, hidden = up.shape
    return call(
        functools.partial(enter_kernel, forward_in), "enter", [struct(rows, hidden + BLK), struct(rows, channels)],
        [flag, *row_halves, *other_halves, gain, up, down], [SMEM] + [VMEM] * 7,
        2 * rows * channels * hidden, 2 * channels * hidden, [pltpu.VMEM((rows, channels), BF16)],
    )


def leave_kernel(forward_in, width, flag, own, got, back_own, back_got, low, high, gain, up, down, *refs):
    kept, sent, scaled, activated, scratch = refs[-5:]

    @pl.when(flag[0] == forward_in)
    def _():
        write_forward(width, own, got, down, kept, sent, scratch)

    @pl.when(flag[0] != forward_in)
    def _():
        write_backward(width, back_own, back_got, own, got, low, high, gain, up, kept, sent, scaled, activated)


def leave(width, forward_in, flag, parts, back_parts, row_halves, gain, up, down, filled, after):
    half, channels = row_halves[0].shape
    hidden = up.shape[1]
    outs = [struct(half, channels, dtype=F32), struct(half, channels), struct(2 * half, hidden), struct(2 * half, hidden)]
    operands = [flag, *parts, *back_parts, *row_halves, gain, up, down, *filled]
    first = len(operands) - len(filled)
    return pl.pallas_call(
        functools.partial(leave_kernel, forward_in, width),
        out_shape=outs,
        in_specs=[SMEM] + [VMEM] * (len(operands) - 1) + [ANY] * len(after),
        out_specs=[VMEM] * 4,
        scratch_shapes=[pltpu.VMEM((2 * half, hidden), BF16)],
        input_output_aliases={first + i: 2 + i for i in range(len(filled))},
        compiler_params=pltpu.CompilerParams(vmem_limit_bytes=12 * MIB),
        cost_estimate=pl.CostEstimate(flops=1, bytes_accessed=1, transcendentals=0),
        name="leave",
    )(*operands, *after)


def block_kernel(channel_blocks, hidden_blocks, depth, capacity, table_counts, plan, gain, *refs):
    *tables, out = refs
    up_count = channel_blocks * hidden_blocks
    dp_index = plan[0, DP]
    z, core = dp_index // 2, lax.rem(dp_index, 2)

    def per_slot(slot, carry):
        owner = 2 * lax.rem(z - lax.rem(slot, depth) + depth, depth) + lax.rem(core + slot // depth, 2)
        number = jnp.int32(-1)
        for entry in range(capacity):
            here = jnp.logical_and(plan[dp_index, OWNERS + entry] == owner, entry < plan[dp_index, COUNT])
            number = jnp.where(here, plan[dp_index, OWNERS + capacity + entry], number)
        is_up = number < up_count
        down_number = jnp.maximum(number - up_count, 0)
        up_number = jnp.maximum(number, 0)
        left_index = jnp.where(is_up, up_number // hidden_blocks, down_number // channel_blocks)
        right_index = jnp.where(is_up, lax.rem(up_number, hidden_blocks), lax.rem(down_number, channel_blocks))
        left = pl.ds(pl.multiple_of(left_index * BLK, BLK), BLK)
        right = pl.ds(pl.multiple_of(right_index * BLK, BLK), BLK)

        def both(halves, cut):
            return jnp.concatenate([half[:, cut] for half in halves], axis=0)

        groups = []
        start = 0
        for count in table_counts:
            groups.append(tables[start : start + count])
            start += count

        def write(is_up_block):
            total = jnp.zeros((BLK, BLK), F32)
            for group in groups:
                rows, scaled, activated, grads = group[:2], group[2], group[3], group[4:]
                if is_up_block:
                    first = (both(rows, left).astype(F32) * gain[:, left].astype(F32)).astype(BF16)
                    second = scaled[:, right]
                else:
                    first = activated[:, left]
                    second = both(grads, right)
                total += lax.dot_general(first, second, (((0,), (0,)), ((), ())), preferred_element_type=F32)
            out[slot] = total.astype(BF16)

        @pl.when(jnp.logical_and(number >= 0, is_up))
        def _():
            write(True)

        @pl.when(jnp.logical_not(is_up))
        def _():
            write(False)

        @pl.when(number < 0)
        def _():
            out[slot] = jnp.zeros((BLK, BLK), BF16)

        return carry

    lax.fori_loop(0, out.shape[0], per_slot, 0)


def outgoing_blocks(plan, capacity, gain, tables, channel_blocks, hidden_blocks):
    slots = lax.axis_size("dp")
    flat = [table for turn in tables for table in turn]
    kernel = functools.partial(
        block_kernel, channel_blocks, hidden_blocks, slots // 2, capacity, [len(turn) for turn in tables]
    )
    return call(
        kernel, "block_grads", [struct(slots, BLK, BLK)], [plan, gain, *flat],
        [SMEM, VMEM] + [VMEM] * len(flat), 4 * slots * BLK * BLK * BLK, 2 * slots * BLK * BLK,
    )[0]


def adam_kernel(depth, plan, relayed, *refs):
    others = refs[: depth - 1]
    first, second, *rest = refs[depth - 1 :]
    outs, (first_new, second_new, direction), sems = rest[-7:-4], rest[-4:-1], rest[-1]
    dp_index = plan[0, DP]
    z, core = dp_index // 2, lax.rem(dp_index, 2)
    slots, capacity = plan.shape[0], first.shape[0]

    def copies(place):
        return [
            pltpu.make_async_copy(new.at[place], out.at[place], sems.at[i, place])
            for i, (new, out) in enumerate(zip((first_new, second_new, direction), outs))
        ]

    def update(place, grad):
        grad = grad.astype(F32)
        first_next = 0.9 * first[place] + 0.1 * grad
        second_next = 0.999 * second[place] + 0.001 * grad * grad
        first_new[place] = first_next
        second_new[place] = second_next
        direction[place] = first_next / (jnp.sqrt(second_next) + 1e-08)
        for copy in copies(place):
            copy.start()

    def per_source(source, place):
        sends = False
        for entry in range(capacity):
            sends = jnp.logical_or(sends, jnp.logical_and(plan[source, OWNERS + entry] == dp_index, entry < plan[source, COUNT]))
        back = lax.rem(source // 2 - z + depth, depth)
        across = lax.rem(source + core, 2)
        for k in range(depth):
            @pl.when(jnp.logical_and(sends, back == k))
            def _():
                if k == 0:
                    update(place, relayed[0])
                else:
                    update(place, others[k - 1][pl.ds(pl.multiple_of(across * BLK, BLK), BLK)])

        return place + jnp.where(sends, 1, 0)

    count = lax.fori_loop(0, slots, per_source, 0)

    def empty(place, carry):
        for new in (first_new, second_new, direction):
            new[place] = jnp.zeros((BLK, BLK), F32)
        for copy in copies(place):
            copy.start()
        return carry

    lax.fori_loop(count, capacity, empty, 0)
    for place in range(capacity):
        for copy in copies(place):
            copy.wait()


def adam(plan, relayed, others, first, second, after):
    shape = jax.ShapeDtypeStruct(first.shape, F32)
    operands = [plan, relayed, *others, first, second]
    return pl.pallas_call(
        functools.partial(adam_kernel, lax.axis_size("dp") // 2),
        out_shape=[shape] * 3,
        in_specs=[SMEM] + [VMEM] * (len(operands) - 1) + [ANY] * len(after),
        out_specs=[HBM] * 3,
        scratch_shapes=[pltpu.VMEM(first.shape, F32)] * 3 + [pltpu.SemaphoreType.DMA((3, first.shape[0]))],
        compiler_params=pltpu.CompilerParams(vmem_limit_bytes=12 * MIB),
        name="adam_step",
    )(*operands, *after)


def finish_kernel(earlier_count, *refs):
    earlier, rows, parts, out = refs[:earlier_count], refs[earlier_count], refs[earlier_count + 1 : -1], refs[-1]
    for turn in range(earlier_count):
        out[turn] = earlier[turn][...]
    total = rows[...].astype(F32)
    for part in parts:
        total += part[...].astype(F32)
    out[earlier_count] = total.astype(BF16)


def finish(earlier, rows, parts):
    operands = [*earlier, rows, *parts]
    return call(
        functools.partial(finish_kernel, len(earlier)), "finish", [struct(len(earlier) + 1, *rows.shape)], operands,
        [VMEM] * len(operands), rows.size, 8 * rows.size,
    )[0]


def finish_pair_kernel(depth, flag, chained, off_grads, off_rows, chain_rows, *refs):
    off_parts, chain_parts, (section_out, grads_out, done) = refs[:depth], refs[depth : 2 * depth], refs[2 * depth :]
    done[...] = jnp.zeros(done.shape, F32)

    def total(local, parts):
        value = local[...].astype(F32)
        for part in parts:
            value += part[...].astype(F32)
        return value.astype(BF16)

    off_back = total(off_grads, [part.at[0] for part in off_parts])
    off_forward = total(off_rows, [part.at[1] for part in off_parts])
    later_turn = total(chain_rows, chain_parts)

    @pl.when(flag[0] == 1)
    def _():
        section_out[0] = chained[...]
        section_out[1] = off_forward
        grads_out[0] = off_back
        grads_out[1] = later_turn

    @pl.when(flag[0] == 0)
    def _():
        section_out[0] = off_forward
        section_out[1] = later_turn
        grads_out[0] = chained[...]
        grads_out[1] = off_back


def finish_pair(flag, chained, off_grads, off_rows, chain_rows, off_parts, chain_parts):
    operands = [flag, chained, off_grads, off_rows, chain_rows, *off_parts, *chain_parts]
    return call(
        functools.partial(finish_pair_kernel, len(off_parts)), "finish_pair",
        [struct(2, *chained.shape)] * 2 + [struct(8, BLK, dtype=F32)], operands,
        [SMEM] + [VMEM] * (len(operands) - 1), 8 * chained.size, 16 * chained.size,
    )


def relay_pair(
    live_rows, arriving, entering, begin, start, stash, gain, up, down, width, plan, exchange
):
    rows = begin.shape[0]
    is_first = lax.axis_index("section") == 0
    flag = is_first.astype(jnp.int32).reshape(1)
    first = first_rows_of(flag, stash, begin, start)
    row_start = lax.axis_index("dp") * rows
    up, down, is_first, row_start, plan = lax.optimization_barrier((up, down, is_first, row_start, plan))

    with jax.named_scope("gather_first"):
        moved = moved_rows(first)
    up = load_one(up, [first, plan])
    with jax.named_scope("gather_first"):
        back_halves, chain_halves = halves(later(moved, up))
    back_product = products(back_halves, gain, up, [])
    down = load_one(down, [back_product])
    with jax.named_scope("swap_back"):
        back_parts = tensor_parts(back_product)
    entered, _ = enter(1, flag, later(chain_halves, back_product), chain_halves, gain, up, down)
    with jax.named_scope("swap_chain0"):
        parts = tensor_parts(entered)
    live = (row_start + lax.iota(jnp.int32, rows) < live_rows[0])[:, None]

    def pick(in_first, in_last):
        return jnp.where(is_first, in_first, in_last)

    others = jnp.stack([
        pick(stash[0], stash[1]),
        pick(start, jnp.where(live, later(arriving, entered)[0], jnp.zeros((), BF16))),
        pick(later(entering, entered)[0], begin),
    ])
    off_grads, off_rows = others[1], others[2]
    with jax.named_scope("gather_others"):
        off_halves, off_grad_halves, off_row_halves = halves(later(moved_rows(later(others, entered)), back_parts[1]))
    off_product = products_and_act_grads(off_halves, off_grad_halves, gain, up, down)
    with jax.named_scope("swap_off_back"):
        off_parts = tensor_parts(off_product)
    off_forward = products(later(off_row_halves, off_product), gain, up, [down])
    with jax.named_scope("swap_off_forward"):
        off_forward_parts = tensor_parts(off_forward)

    with jax.named_scope("chain0"):
        kept, sent, scaled, activated = leave(
            width, 1, flag, parts, back_parts, back_halves, gain, up, down, [], [off_product, off_forward]
        )
        chained = added(first[1], scatter_parts(scatter_pairs(kept, sent)))
    with jax.named_scope("off_back"):
        kept, sent, off_scaled, off_activated = joint_backward(width, off_parts, off_halves, gain, up, down, [])
        off_back_pairs = scatter_pairs(kept, sent)
    with jax.named_scope("pass"):
        passed = later(halves(moved_passed(chained))[0], kept)
    chain_in = passed[0][:rows]
    entered, grads = enter(0, flag, passed, chain_halves, gain, up, down)
    with jax.named_scope("swap_chain1"):
        parts = tensor_parts(entered)
    with jax.named_scope("off_forward"):
        kept, sent = forward(width, off_forward_parts, up, down, [entered])
        pairs = jnp.stack([off_back_pairs, scatter_pairs(kept, sent)], axis=1)
        off_sums = scatter_parts(pairs)
    with jax.named_scope("chain1"):
        kept, sent, scaled, activated = leave(
            width, 0, flag, parts, back_parts, back_halves, gain, up, down, [scaled, activated], [pairs]
        )
        got = sibling(sent)
        chain_sums = scatter_parts(summed_pairs(kept, got))
    tables = [
        (*back_halves, scaled, activated, grads),
        (*off_halves, off_scaled, off_activated, *off_grad_halves),
    ]
    relayed, from_others, off_sums = exchange(plan, tables, got, off_sums)
    section_outputs, input_grads, done = finish_pair(
        flag, chained, off_grads, off_rows, chain_in, off_sums, chain_sums
    )
    return section_outputs, input_grads, plan, relayed, from_others, [done]


def relay(
    is_first, is_last, masked, entering, section_inputs, grad_outputs, stashed_inputs, gain, up, down, width
):
    turn_count = stashed_inputs.shape[1]
    local_rows = section_inputs.shape[1]
    up, down, is_first, is_last, masked = lax.optimization_barrier((up, down, is_first, is_last, masked))
    grads_in, rows_in = grad_outputs[0], section_inputs[0]
    first = jnp.concatenate([stashed_inputs[0, :1], grad_outputs])
    with jax.named_scope("gather_first"):
        moved = moved_rows(first)
    up, down = load_weights(up, down, first)
    with jax.named_scope("gather_first"):
        gathered = halves(later(moved, up))
    stash_rows = [gathered[0]]
    grad_halves = gathered[1]
    back_products = [products(stash_rows[0], gain, up, [down])]
    with jax.named_scope("swap_b0p"):
        back_parts = [tensor_parts(back_products[0])]
    act_grad = act_grads(later(grad_halves, back_products[0]), up, down)
    with jax.named_scope("swap_b0a"):
        act_parts = tensor_parts(act_grad)
    with jax.named_scope("gather_others"):
        others = jnp.concatenate([section_inputs, stashed_inputs[0, 1:]])
        gathered = halves(moved_rows(later(others, act_grad)))
    product = products(gathered[0], gain, up, [down])
    with jax.named_scope("swap_f0p"):
        parts = tensor_parts(product)
    ahead = [product]
    for turn in range(1, turn_count):
        stash_rows.append(gathered[turn])
        back_products.append(products(stash_rows[turn], gain, up, [down]))
        ahead.append(back_products[turn])
        with jax.named_scope("swap_b1p"):
            back_parts.append(tensor_parts(back_products[turn]))

    forward_results = []
    backward_results = []
    tables = []
    for turn in range(turn_count):
        with jax.named_scope(f"backward{turn}"):
            kept, sent, scaled, activated = backward(
                width, back_parts[turn], act_parts, stash_rows[turn], gain, up, down, ahead
            )
            back_pairs = scatter_pairs(kept, sent)
        tables.append((*stash_rows[turn], scaled, activated, *grad_halves))
        if turn + 1 == turn_count:
            with jax.named_scope(f"backward{turn}"):
                back_sums = scatter_parts(back_pairs)
            parts = later(parts, back_sums)
        with jax.named_scope(f"forward{turn}"):
            kept, sent = forward(width, parts, up, down, [])
            pairs = scatter_pairs(kept, sent)
        if turn + 1 == turn_count:
            with jax.named_scope(f"forward{turn}"):
                sums = scatter_parts(pairs)
            input_grads = finish(backward_results, grads_in, back_sums)
            section_outputs = finish(forward_results, rows_in, sums)
            break
        with jax.named_scope(f"scatter{turn}"):
            sums = scatter_parts(jnp.stack([back_pairs, pairs], axis=1))
        backward_results.append(added(grads_in, [part[0] for part in sums]))
        forward_results.append(added(rows_in, [part[1] for part in sums]))
        with jax.named_scope(f"gather{turn}"):
            moved = moved_passed(
                jnp.where(is_first, masked[turn], backward_results[-1]),
                jnp.where(is_last, entering[turn], forward_results[-1]),
            )
            passed = halves(later(moved, back_parts[turn + 1][1]))
        grad_halves = passed[0]
        grads_in, rows_in = passed[0][0][:local_rows], passed[1][0][:local_rows]
        act_grad = act_grads(grad_halves, up, down)
        with jax.named_scope("swap_b1a"):
            act_parts = tensor_parts(act_grad)
        product = products(later(passed[1], act_grad), gain, up, [down])
        with jax.named_scope("swap_f1p"):
            parts = tensor_parts(product)
        ahead = []
    return section_outputs, input_grads, tables


def body(
    section_inputs,
    entering,
    grad_outputs,
    arriving,
    live_rows,
    stashed_inputs,
    norm_gain,
    up_weight,
    down_weight,
    held_blocks,
    held_count,
    held_owner,
    first_moment,
    second_moment,
):
    section_count = lax.axis_size("section")
    section_index = lax.axis_index("section")
    dp_count = lax.axis_size("dp")
    turn_count = stashed_inputs.shape[1]
    local_rows = section_inputs.shape[1]
    channels, hidden = up_weight.shape[1:]
    width = channels * lax.axis_size("tensor")
    is_first = section_index == 0
    is_last = section_index == section_count - 1
    counts, owners, blocks = held_count[0, 0], held_owner[0, 0], held_blocks[0, 0]
    capacity = owners.shape[1]
    dp_index = lax.axis_index("dp")
    plan = jnp.concatenate([jnp.full((dp_count, 1), dp_index, jnp.int32), counts[:, None], owners, blocks], axis=1)

    def exchange(plan, tables, before, beside):
        with jax.named_scope("block_exchange"):
            outgoing = outgoing_blocks(plan, capacity, norm_gain, tables, channels // BLK, hidden // BLK)
            outgoing = outgoing.reshape((2, dp_count // 2, BLK, BLK))
            beside = later(beside, outgoing)
            relayed = later(sibling(outgoing[1]), before, beside)
            pairs = [jnp.concatenate([outgoing[0, k], relayed[k]]) for k in range(1, dp_count // 2)]
            return relayed, [shifted(pair, -k - 1) for k, pair in enumerate(pairs)], beside

    if section_count == 2 and turn_count == 2:
        section_outputs, input_grads, plan, relayed, others, after = relay_pair(
            live_rows, arriving, entering, section_inputs[0], grad_outputs[0], stashed_inputs[0], norm_gain,
            up_weight[0], down_weight[0], width, plan, exchange,
        )
    else:
        row_ids = dp_index * local_rows + lax.iota(jnp.int32, local_rows)
        masked = jnp.where((row_ids < live_rows[:, None])[..., None], arriving, jnp.zeros((), BF16))
        section_outputs, input_grads, tables = relay(
            is_first, is_last, masked, entering, section_inputs, grad_outputs, stashed_inputs, norm_gain,
            up_weight[0], down_weight[0], width,
        )
        relayed, others, _ = exchange(plan, tables, None, None)
        after = []
    first_out, second_out, direction_out = adam(
        plan, relayed, others, first_moment[0, 0, 0], second_moment[0, 0, 0], after
    )
    return (
        section_outputs[None],
        input_grads[None],
        first_out[None, None, None],
        second_out[None, None, None],
        direction_out[None, None, None],
    )


def solution(mesh):
    return jax.shard_map(
        body,
        mesh=mesh,
        in_specs=(
            P("section", "dp", "tensor"),
            P(None, "dp", "tensor"),
            P("section", "dp", "tensor"),
            P(None, "dp", "tensor"),
            P(),
            P("section", None, "dp", "tensor"),
            P("section", "tensor"),
            P("section", "tensor", "dp"),
            P("section", "dp", "tensor"),
            P("section", "tensor", None, None),
            P("section", "tensor", None),
            P("section", "tensor", None, None),
            P("section", "tensor", "dp", None, None, None),
            P("section", "tensor", "dp", None, None, None),
        ),
        out_specs=(
            P("section", None, "dp", "tensor"),
            P("section", None, "dp", "tensor"),
            P("section", "tensor", "dp", None, None, None),
            P("section", "tensor", "dp", None, None, None),
            P("section", "tensor", "dp", None, None, None),
        ),
        check_vma=False,
    )
```

```python
import functools

import jax
import jax.numpy as jnp
from jax import lax
from jax.experimental import pallas as pl
from jax.experimental.pallas import tpu as pltpu
from jax.sharding import PartitionSpec as P

BLK = 128
EPSILON = 1e-06
BF16 = jnp.bfloat16
F32 = jnp.float32
MIB = 1024 * 1024
VMEM = pl.BlockSpec(memory_space=pltpu.VMEM)
SMEM = pl.BlockSpec(memory_space=pltpu.SMEM)
HBM = pl.BlockSpec(memory_space=pltpu.HBM)
ANY = pl.BlockSpec(memory_space=pl.ANY)
DP, COUNT, OWNERS = range(3)


def later(values, *before):
    return lax.optimization_barrier((values, before))[0]


def sibling(value):
    return lax.ppermute(value, "dp", [(d, d ^ 1) for d in range(lax.axis_size("dp"))])


def shifted(value, steps):
    count = lax.axis_size("dp")
    return lax.ppermute(value, "dp", [(d, (d + 2 * steps) % count) for d in range(count)])


def moved_rows(local):
    depth = lax.axis_size("dp") // 2
    return [local] + [shifted(local, k) for k in range(1, depth)]


def moved_passed(down, up=None):
    sections = lax.axis_size("section")
    count = lax.axis_size("dp")

    def moved(local, direction, k):
        pairs = [
            (s * count + d, (s + direction) % sections * count + (d + 2 * k) % count)
            for s in range(sections)
            for d in range(count)
        ]
        return lax.ppermute(local, ("section", "dp"), pairs)

    both = down[None] if up is None else jnp.stack([down, up])
    if sections == 2:
        return [moved(both, 1, k) for k in range(count // 2)]
    return [jnp.stack([moved(down, -1, k), moved(up, 1, k)]) for k in range(count // 2)]


def halves(pieces):
    mine = [jnp.concatenate([piece[i] for piece in pieces]) for i in range(pieces[0].shape[0])]
    return [[half, sibling(half)] for half in mine]


def scatter_pairs(kept, sent):
    return summed_pairs(kept, sibling(sent))


def summed_pairs(kept, got):
    depth = lax.axis_size("dp") // 2
    return (kept + got.astype(F32)).reshape((depth, kept.shape[0] // depth, kept.shape[1]))


def scatter_parts(pairs):
    return [pairs[0]] + [shifted(pairs[k].astype(BF16), -k) for k in range(1, pairs.shape[0])]


def added(rows, parts):
    return sum([part.astype(F32) for part in parts], rows.astype(F32)).astype(BF16)


def tensor_parts(value):
    count = lax.axis_size("tensor")
    step = 1
    while True:
        got = lax.ppermute(value, "tensor", [(t, t ^ step) for t in range(count)])
        step *= 2
        if step >= count:
            return value, got
        value = value + got


def tile_of(size):
    return 256 if size % 256 == 0 else BLK


def call(kernel, name, outs, operands, specs, flops, moved, scratch=()):
    return pl.pallas_call(
        kernel,
        out_shape=outs,
        in_specs=specs,
        out_specs=[VMEM] * len(outs),
        scratch_shapes=scratch,
        compiler_params=pltpu.CompilerParams(vmem_limit_bytes=12 * MIB),
        cost_estimate=pl.CostEstimate(flops=1, bytes_accessed=1, transcendentals=0),
        name=name,
    )(*operands)


def struct(*shape, dtype=BF16):
    return jax.ShapeDtypeStruct(shape, dtype)


def nt_dot(left, right):
    return lax.dot_general(left, right, (((1,), (1,)), ((), ())), preferred_element_type=F32)


def load_kernel(up_in, down_in, after, up, down, sems):
    copies = [pltpu.make_async_copy(up_in, up, sems.at[0]), pltpu.make_async_copy(down_in, down, sems.at[1])]
    for copy in copies:
        copy.start()
    for copy in copies:
        copy.wait()


def load_one_kernel(source, *refs):
    target, sem = refs[-2:]
    copy = pltpu.make_async_copy(source, target, sem)
    copy.start()
    copy.wait()


def load_one(weight, after):
    return pl.pallas_call(
        load_one_kernel,
        out_shape=pltpu.VMEM(weight.shape, BF16),
        in_specs=[HBM] + [ANY] * len(after),
        out_specs=VMEM,
        scratch_shapes=[pltpu.SemaphoreType.DMA(())],
        compiler_params=pltpu.CompilerParams(vmem_limit_bytes=8 * MIB),
        name="load_weight",
    )(in_hbm(weight), *after)


def first_kernel(flag, stash, begin, start, out, sems):
    stashed = pltpu.make_async_copy(stash.at[flag[0]], out.at[0], sems.at[0])
    stashed.start()

    @pl.when(flag[0] == 1)
    def _():
        copy = pltpu.make_async_copy(begin, out.at[1], sems.at[1])
        copy.start()
        copy.wait()

    @pl.when(flag[0] == 0)
    def _():
        copy = pltpu.make_async_copy(start, out.at[1], sems.at[1])
        copy.start()
        copy.wait()

    stashed.wait()


def first_rows_of(flag, stash, begin, start):
    return pl.pallas_call(
        first_kernel,
        out_shape=struct(2, *begin.shape),
        in_specs=[SMEM] + [HBM] * 3,
        out_specs=VMEM,
        scratch_shapes=[pltpu.SemaphoreType.DMA((2,))],
        compiler_params=pltpu.CompilerParams(vmem_limit_bytes=2 * MIB),
        name="first_rows",
    )(flag, *map(in_hbm, [stash, begin, start]))


def load_weights(up, down, after):
    return pl.pallas_call(
        load_kernel,
        out_shape=[pltpu.VMEM(up.shape, BF16), pltpu.VMEM(down.shape, BF16)],
        in_specs=[HBM] * 2 + [ANY],
        out_specs=[VMEM] * 2,
        scratch_shapes=[pltpu.SemaphoreType.DMA((2,))],
        compiler_params=pltpu.CompilerParams(vmem_limit_bytes=16 * MIB),
        name="load_weights",
    )(in_hbm(up), in_hbm(down), after)


def in_hbm(value):
    return pltpu.with_memory_space_constraint(value, pltpu.HBM)


def write_products(rows, gain, up, sent, normed):
    widened = rows.astype(F32)
    squares = jnp.sum(widened * widened, axis=1, keepdims=True)
    normed[...] = (widened * gain[...].astype(F32)).astype(BF16)
    hidden = up.shape[1]
    step = tile_of(hidden)
    for n in range(0, hidden, step):
        sent[:, n : n + step] = jnp.dot(normed[...], up[:, n : n + step], preferred_element_type=F32).astype(BF16)
    coarse = squares.astype(BF16).astype(F32)
    lane = lax.broadcasted_iota(jnp.int32, (rows.shape[0], BLK), 1)
    sent[:, hidden:] = jnp.where(lane == 0, coarse, jnp.where(lane == 1, squares - coarse, 0.0)).astype(BF16)


def write_act_grads(grads, down, sent):
    hidden = down.shape[0]
    step = tile_of(hidden)
    for n in range(0, hidden, step):
        sent[:, n : n + step] = nt_dot(grads[...], down[n : n + step, :]).astype(BF16)


def joined(low, high):
    return jnp.concatenate([low[...], high[...]], axis=0)


def product_kernel(low, high, gain, up, *refs):
    sent, normed = refs[-2:]
    write_products(joined(low, high), gain, up, sent, normed)


def products(row_halves, gain, up, down):
    rows = 2 * row_halves[0].shape[0]
    channels, hidden = up.shape
    operands = [*row_halves, gain, up, *down]
    return call(
        product_kernel, "products", [struct(rows, hidden + BLK)],
        operands, [VMEM] * len(operands), 2 * rows * channels * hidden, 2 * channels * hidden,
        [pltpu.VMEM((rows, channels), BF16)],
    )[0]


def act_kernel(low, high, down, _, sent, grads):
    grads[...] = joined(low, high)
    write_act_grads(grads, down, sent)


def act_grads(grad_halves, up, down):
    rows = 2 * grad_halves[0].shape[0]
    hidden, channels = down.shape
    return call(
        act_kernel, "act_grads", [struct(rows, hidden)],
        [*grad_halves, down, up], [VMEM] * 4, 2 * rows * channels * hidden, 2 * channels * hidden,
        [pltpu.VMEM((rows, channels), BF16)],
    )[0]


def product_act_kernel(low, high, grad_low, grad_high, gain, up, down, sent, normed):
    width = up.shape[1] + BLK
    write_products(joined(low, high), gain, up, sent.at[:, :width], normed)
    normed[...] = joined(grad_low, grad_high)
    write_act_grads(normed, down, sent.at[:, width:])


def products_and_act_grads(row_halves, grad_halves, gain, up, down):
    rows = 2 * row_halves[0].shape[0]
    channels, hidden = up.shape
    return call(
        product_act_kernel, "products_and_act_grads", [struct(rows, 2 * hidden + BLK)],
        [*row_halves, *grad_halves, gain, up, down], [VMEM] * 7, 4 * rows * channels * hidden, 4 * channels * hidden,
        [pltpu.VMEM((rows, channels), BF16)],
    )[0]


def scales_in(own, got, hidden, width):
    tail = own[:, hidden:].astype(F32) + got[:, hidden:].astype(F32)
    return lax.rsqrt((tail[:, 0:1] + tail[:, 1:2]) / width + EPSILON)


def gate_of(hidden):
    return 1.0 / (1.0 + jnp.exp(-hidden))


def write_backward(width, own, got, act_own, act_got, low, high, gain, up, kept, sent, scaled, activated):
    channels, hidden = up.shape
    scales = scales_in(own, got, hidden, width)
    scale_grad = jnp.zeros_like(scales)
    step = tile_of(hidden)
    for n in range(0, hidden, step):
        cut = slice(n, n + step)
        product = own[:, cut].astype(F32) + got[:, cut].astype(F32)
        act_grad = act_own[:, cut].astype(F32) + act_got[:, cut].astype(F32)
        value = product * scales
        gate = gate_of(value)
        activated[:, cut] = (value * gate).astype(BF16)
        grad = act_grad * gate * (1.0 + value * (1.0 - gate))
        scaled[:, cut] = (grad * scales).astype(BF16)
        scale_grad += jnp.sum(grad * product, axis=1, keepdims=True)
    factor = scale_grad * scales * scales * scales / width
    half = low.shape[0]
    step = tile_of(channels)
    for c in range(0, channels, step):
        cut = slice(c, c + step)
        part = nt_dot(scaled[...], up[cut, :]) * gain[:, cut].astype(F32)
        kept[:, cut] = part[:half] - factor[:half] * low[:, cut].astype(F32)
        sent[:, cut] = (part[half:] - factor[half:] * high[:, cut].astype(F32)).astype(BF16)


def write_forward(width, own, got, down, kept, sent, activated):
    hidden, channels = down.shape
    scales = scales_in(own, got, hidden, width)
    step = tile_of(hidden)
    for n in range(0, hidden, step):
        cut = slice(n, n + step)
        value = (own[:, cut].astype(F32) + got[:, cut].astype(F32)) * scales
        activated[:, cut] = (value * gate_of(value)).astype(BF16)
    half = kept.shape[0]
    step = tile_of(channels)
    for c in range(0, channels, step):
        cut = slice(c, c + step)
        part = jnp.dot(activated[...], down[:, cut], preferred_element_type=F32)
        kept[:, cut] = part[:half]
        sent[:, cut] = part[half:].astype(BF16)


def backward_kernel(width, own, got, act_own, act_got, low, high, gain, up, _, *refs):
    write_backward(width, own, got, act_own, act_got, low, high, gain, up, *refs[-4:])


def joint_backward_kernel(width, own, got, low, high, gain, up, _, *refs):
    cut = up.shape[1] + BLK
    write_backward(
        width, own.at[:, :cut], got.at[:, :cut], own.at[:, cut:], got.at[:, cut:], low, high, gain, up, *refs[-4:]
    )


def joint_backward(width, parts, row_halves, gain, up, down, after):
    half, channels = row_halves[0].shape
    hidden = up.shape[1]
    outs = [struct(half, channels, dtype=F32), struct(half, channels), struct(2 * half, hidden), struct(2 * half, hidden)]
    operands = [*parts, *row_halves, gain, up, down]
    return call(
        functools.partial(joint_backward_kernel, width), "backward", outs, operands + after,
        [VMEM] * len(operands) + [ANY] * len(after),
        4 * half * channels * hidden, 2 * channels * hidden,
    )


def backward(width, products_parts, act_parts, row_halves, gain, up, down, after):
    half, channels = row_halves[0].shape
    hidden = up.shape[1]
    outs = [struct(half, channels, dtype=F32), struct(half, channels), struct(2 * half, hidden), struct(2 * half, hidden)]
    operands = [*products_parts, *act_parts, *row_halves, gain, up, down]
    return call(
        functools.partial(backward_kernel, width), "backward", outs, operands + after,
        [VMEM] * len(operands) + [ANY] * len(after),
        4 * half * channels * hidden, 2 * channels * hidden,
    )


def forward_kernel(width, own, got, down, _, *refs):
    write_forward(width, own, got, down, *refs[-3:])


def forward(width, products_parts, up, down, after):
    rows = products_parts[0].shape[0]
    hidden, channels = down.shape
    outs = [struct(rows // 2, channels, dtype=F32), struct(rows // 2, channels)]
    return call(
        functools.partial(forward_kernel, width), "forward", outs, [*products_parts, down, up, *after],
        [VMEM] * 4 + [ANY] * len(after),
        2 * rows * channels * hidden, 2 * channels * hidden, [pltpu.VMEM((rows, hidden), BF16)],
    )


def enter_kernel(forward_in, flag, low, high, other_low, other_high, gain, up, down, sent, grads, normed):
    @pl.when(flag[0] == forward_in)
    def _():
        write_products(joined(low, high), gain, up, sent, normed)
        grads[...] = joined(other_low, other_high)

    @pl.when(flag[0] != forward_in)
    def _():
        grads[...] = joined(low, high)
        write_act_grads(grads, down, sent)
        sent[:, up.shape[1] :] = jnp.zeros((sent.shape[0], BLK), BF16)


def enter(forward_in, flag, row_halves, other_halves, gain, up, down):
    rows = 2 * row_halves[0].shape[0]
    channels, hidden = up.shape
    return call(
        functools.partial(enter_kernel, forward_in), "enter", [struct(rows, hidden + BLK), struct(rows, channels)],
        [flag, *row_halves, *other_halves, gain, up, down], [SMEM] + [VMEM] * 7,
        2 * rows * channels * hidden, 2 * channels * hidden, [pltpu.VMEM((rows, channels), BF16)],
    )


def leave_kernel(forward_in, width, flag, own, got, back_own, back_got, low, high, gain, up, down, *refs):
    kept, sent, scaled, activated, scratch = refs[-5:]

    @pl.when(flag[0] == forward_in)
    def _():
        write_forward(width, own, got, down, kept, sent, scratch)

    @pl.when(flag[0] != forward_in)
    def _():
        write_backward(width, back_own, back_got, own, got, low, high, gain, up, kept, sent, scaled, activated)


def leave(width, forward_in, flag, parts, back_parts, row_halves, gain, up, down, filled, after):
    half, channels = row_halves[0].shape
    hidden = up.shape[1]
    outs = [struct(half, channels, dtype=F32), struct(half, channels), struct(2 * half, hidden), struct(2 * half, hidden)]
    operands = [flag, *parts, *back_parts, *row_halves, gain, up, down, *filled]
    first = len(operands) - len(filled)
    return pl.pallas_call(
        functools.partial(leave_kernel, forward_in, width),
        out_shape=outs,
        in_specs=[SMEM] + [VMEM] * (len(operands) - 1) + [ANY] * len(after),
        out_specs=[VMEM] * 4,
        scratch_shapes=[pltpu.VMEM((2 * half, hidden), BF16)],
        input_output_aliases={first + i: 2 + i for i in range(len(filled))},
        compiler_params=pltpu.CompilerParams(vmem_limit_bytes=12 * MIB),
        cost_estimate=pl.CostEstimate(flops=1, bytes_accessed=1, transcendentals=0),
        name="leave",
    )(*operands, *after)


def block_kernel(channel_blocks, hidden_blocks, depth, capacity, table_counts, plan, gain, *refs):
    *tables, out = refs
    up_count = channel_blocks * hidden_blocks
    dp_index = plan[0, DP]
    z, core = dp_index // 2, lax.rem(dp_index, 2)

    def per_slot(slot, carry):
        owner = 2 * lax.rem(z - lax.rem(slot, depth) + depth, depth) + lax.rem(core + slot // depth, 2)
        number = jnp.int32(-1)
        for entry in range(capacity):
            here = jnp.logical_and(plan[dp_index, OWNERS + entry] == owner, entry < plan[dp_index, COUNT])
            number = jnp.where(here, plan[dp_index, OWNERS + capacity + entry], number)
        is_up = number < up_count
        down_number = jnp.maximum(number - up_count, 0)
        up_number = jnp.maximum(number, 0)
        left_index = jnp.where(is_up, up_number // hidden_blocks, down_number // channel_blocks)
        right_index = jnp.where(is_up, lax.rem(up_number, hidden_blocks), lax.rem(down_number, channel_blocks))
        left = pl.ds(pl.multiple_of(left_index * BLK, BLK), BLK)
        right = pl.ds(pl.multiple_of(right_index * BLK, BLK), BLK)

        def both(halves, cut):
            return jnp.concatenate([half[:, cut] for half in halves], axis=0)

        groups = []
        start = 0
        for count in table_counts:
            groups.append(tables[start : start + count])
            start += count

        def write(is_up_block):
            total = jnp.zeros((BLK, BLK), F32)
            for group in groups:
                rows, scaled, activated, grads = group[:2], group[2], group[3], group[4:]
                if is_up_block:
                    first = (both(rows, left).astype(F32) * gain[:, left].astype(F32)).astype(BF16)
                    second = scaled[:, right]
                else:
                    first = activated[:, left]
                    second = both(grads, right)
                total += lax.dot_general(first, second, (((0,), (0,)), ((), ())), preferred_element_type=F32)
            out[slot] = total.astype(BF16)

        @pl.when(jnp.logical_and(number >= 0, is_up))
        def _():
            write(True)

        @pl.when(jnp.logical_not(is_up))
        def _():
            write(False)

        @pl.when(number < 0)
        def _():
            out[slot] = jnp.zeros((BLK, BLK), BF16)

        return carry

    lax.fori_loop(0, out.shape[0], per_slot, 0)


def outgoing_blocks(plan, capacity, gain, tables, channel_blocks, hidden_blocks):
    slots = lax.axis_size("dp")
    flat = [table for turn in tables for table in turn]
    kernel = functools.partial(
        block_kernel, channel_blocks, hidden_blocks, slots // 2, capacity, [len(turn) for turn in tables]
    )
    return call(
        kernel, "block_grads", [struct(slots, BLK, BLK)], [plan, gain, *flat],
        [SMEM, VMEM] + [VMEM] * len(flat), 4 * slots * BLK * BLK * BLK, 2 * slots * BLK * BLK,
    )[0]


def adam_kernel(depth, plan, relayed, *refs):
    others = refs[: depth - 1]
    first, second, *rest = refs[depth - 1 :]
    outs, (first_new, second_new, direction), sems = rest[-7:-4], rest[-4:-1], rest[-1]
    dp_index = plan[0, DP]
    z, core = dp_index // 2, lax.rem(dp_index, 2)
    slots, capacity = plan.shape[0], first.shape[0]

    def copies(place):
        return [
            pltpu.make_async_copy(new.at[place], out.at[place], sems.at[i, place])
            for i, (new, out) in enumerate(zip((first_new, second_new, direction), outs))
        ]

    def update(place, grad):
        grad = grad.astype(F32)
        first_next = 0.9 * first[place] + 0.1 * grad
        second_next = 0.999 * second[place] + 0.001 * grad * grad
        first_new[place] = first_next
        second_new[place] = second_next
        direction[place] = first_next / (jnp.sqrt(second_next) + 1e-08)
        for copy in copies(place):
            copy.start()

    def per_source(source, place):
        sends = False
        for entry in range(capacity):
            sends = jnp.logical_or(sends, jnp.logical_and(plan[source, OWNERS + entry] == dp_index, entry < plan[source, COUNT]))
        back = lax.rem(source // 2 - z + depth, depth)
        across = lax.rem(source + core, 2)
        for k in range(depth):
            @pl.when(jnp.logical_and(sends, back == k))
            def _():
                if k == 0:
                    update(place, relayed[0])
                else:
                    update(place, others[k - 1][pl.ds(pl.multiple_of(across * BLK, BLK), BLK)])

        return place + jnp.where(sends, 1, 0)

    count = lax.fori_loop(0, slots, per_source, 0)

    def empty(place, carry):
        for new in (first_new, second_new, direction):
            new[place] = jnp.zeros((BLK, BLK), F32)
        for copy in copies(place):
            copy.start()
        return carry

    lax.fori_loop(count, capacity, empty, 0)
    for place in range(capacity):
        for copy in copies(place):
            copy.wait()


def adam(plan, relayed, others, first, second, after):
    shape = jax.ShapeDtypeStruct(first.shape, F32)
    operands = [plan, relayed, *others, first, second]
    return pl.pallas_call(
        functools.partial(adam_kernel, lax.axis_size("dp") // 2),
        out_shape=[shape] * 3,
        in_specs=[SMEM] + [VMEM] * (len(operands) - 1) + [ANY] * len(after),
        out_specs=[HBM] * 3,
        scratch_shapes=[pltpu.VMEM(first.shape, F32)] * 3 + [pltpu.SemaphoreType.DMA((3, first.shape[0]))],
        compiler_params=pltpu.CompilerParams(vmem_limit_bytes=12 * MIB),
        name="adam_step",
    )(*operands, *after)


def finish_kernel(earlier_count, *refs):
    earlier, rows, parts, out = refs[:earlier_count], refs[earlier_count], refs[earlier_count + 1 : -1], refs[-1]
    for turn in range(earlier_count):
        out[turn] = earlier[turn][...]
    total = rows[...].astype(F32)
    for part in parts:
        total += part[...].astype(F32)
    out[earlier_count] = total.astype(BF16)


def finish(earlier, rows, parts):
    operands = [*earlier, rows, *parts]
    return call(
        functools.partial(finish_kernel, len(earlier)), "finish", [struct(len(earlier) + 1, *rows.shape)], operands,
        [VMEM] * len(operands), rows.size, 8 * rows.size,
    )[0]


def finish_pair_kernel(depth, flag, chained, off_grads, off_rows, chain_rows, *refs):
    off_parts, chain_parts, (section_out, grads_out, done) = refs[:depth], refs[depth : 2 * depth], refs[2 * depth :]
    done[...] = jnp.zeros(done.shape, F32)

    def total(local, parts):
        value = local[...].astype(F32)
        for part in parts:
            value += part[...].astype(F32)
        return value.astype(BF16)

    off_back = total(off_grads, [part.at[0] for part in off_parts])
    off_forward = total(off_rows, [part.at[1] for part in off_parts])
    later_turn = total(chain_rows, chain_parts)

    @pl.when(flag[0] == 1)
    def _():
        section_out[0] = chained[...]
        section_out[1] = off_forward
        grads_out[0] = off_back
        grads_out[1] = later_turn

    @pl.when(flag[0] == 0)
    def _():
        section_out[0] = off_forward
        section_out[1] = later_turn
        grads_out[0] = chained[...]
        grads_out[1] = off_back


def finish_pair(flag, chained, off_grads, off_rows, chain_rows, off_parts, chain_parts):
    operands = [flag, chained, off_grads, off_rows, chain_rows, *off_parts, *chain_parts]
    return call(
        functools.partial(finish_pair_kernel, len(off_parts)), "finish_pair",
        [struct(2, *chained.shape)] * 2 + [struct(8, BLK, dtype=F32)], operands,
        [SMEM] + [VMEM] * (len(operands) - 1), 8 * chained.size, 16 * chained.size,
    )


def relay_pair(
    live_rows, arriving, entering, begin, start, stash, gain, up, down, width, plan, exchange
):
    rows = begin.shape[0]
    is_first = lax.axis_index("section") == 0
    flag = is_first.astype(jnp.int32).reshape(1)
    first = first_rows_of(flag, stash, begin, start)
    row_start = lax.axis_index("dp") * rows
    up, down, is_first, row_start, plan = lax.optimization_barrier((up, down, is_first, row_start, plan))

    with jax.named_scope("gather_first"):
        moved = moved_rows(first)
    up = load_one(up, [first, plan])
    with jax.named_scope("gather_first"):
        back_halves, chain_halves = halves(later(moved, up))
    back_product = products(back_halves, gain, up, [])
    down = load_one(down, [back_product])
    with jax.named_scope("swap_back"):
        back_parts = tensor_parts(back_product)
    entered, _ = enter(1, flag, later(chain_halves, back_product), chain_halves, gain, up, down)
    with jax.named_scope("swap_chain0"):
        parts = tensor_parts(entered)
    live = (row_start + lax.iota(jnp.int32, rows) < live_rows[0])[:, None]

    def pick(in_first, in_last):
        return jnp.where(is_first, in_first, in_last)

    others = jnp.stack([
        pick(stash[0], stash[1]),
        pick(start, jnp.where(live, later(arriving, entered)[0], jnp.zeros((), BF16))),
        pick(later(entering, entered)[0], begin),
    ])
    off_grads, off_rows = others[1], others[2]
    with jax.named_scope("gather_others"):
        off_halves, off_grad_halves, off_row_halves = halves(later(moved_rows(later(others, entered)), back_parts[1]))
    off_product = products_and_act_grads(off_halves, off_grad_halves, gain, up, down)
    with jax.named_scope("swap_off_back"):
        off_parts = tensor_parts(off_product)
    off_forward = products(later(off_row_halves, off_product), gain, up, [down])
    with jax.named_scope("swap_off_forward"):
        off_forward_parts = tensor_parts(off_forward)

    with jax.named_scope("chain0"):
        kept, sent, scaled, activated = leave(
            width, 1, flag, parts, back_parts, back_halves, gain, up, down, [], [off_product]
        )
        chained = added(first[1], scatter_parts(scatter_pairs(kept, sent)))
    with jax.named_scope("off_back"):
        kept, sent, off_scaled, off_activated = joint_backward(width, off_parts, off_halves, gain, up, down, [])
        off_back_pairs = scatter_pairs(kept, sent)
    with jax.named_scope("pass"):
        passed = later(halves(moved_passed(chained))[0], kept)
    chain_in = passed[0][:rows]
    entered, grads = enter(0, flag, passed, chain_halves, gain, up, down)
    with jax.named_scope("swap_chain1"):
        parts = tensor_parts(entered)
    with jax.named_scope("off_forward"):
        kept, sent = forward(width, off_forward_parts, up, down, [entered])
        pairs = jnp.stack([off_back_pairs, scatter_pairs(kept, sent)], axis=1)
        off_sums = scatter_parts(pairs)
    with jax.named_scope("chain1"):
        kept, sent, scaled, activated = leave(
            width, 0, flag, parts, back_parts, back_halves, gain, up, down, [scaled, activated], [pairs]
        )
        got = sibling(sent)
        chain_sums = scatter_parts(summed_pairs(kept, got))
        off_sums = later(off_sums, kept)
    tables = [
        (*back_halves, scaled, activated, grads),
        (*off_halves, off_scaled, off_activated, *off_grad_halves),
    ]
    relayed, from_others = exchange(later(plan, off_sums), tables, got)
    section_outputs, input_grads, done = finish_pair(
        flag, chained, off_grads, off_rows, chain_in, off_sums, chain_sums
    )
    return section_outputs, input_grads, plan, relayed, from_others, [done]


def relay(
    is_first, is_last, masked, entering, section_inputs, grad_outputs, stashed_inputs, gain, up, down, width
):
    turn_count = stashed_inputs.shape[1]
    local_rows = section_inputs.shape[1]
    up, down, is_first, is_last, masked = lax.optimization_barrier((up, down, is_first, is_last, masked))
    grads_in, rows_in = grad_outputs[0], section_inputs[0]
    first = jnp.concatenate([stashed_inputs[0, :1], grad_outputs])
    with jax.named_scope("gather_first"):
        moved = moved_rows(first)
    up, down = load_weights(up, down, first)
    with jax.named_scope("gather_first"):
        gathered = halves(later(moved, up))
    stash_rows = [gathered[0]]
    grad_halves = gathered[1]
    back_products = [products(stash_rows[0], gain, up, [down])]
    with jax.named_scope("swap_b0p"):
        back_parts = [tensor_parts(back_products[0])]
    act_grad = act_grads(later(grad_halves, back_products[0]), up, down)
    with jax.named_scope("swap_b0a"):
        act_parts = tensor_parts(act_grad)
    with jax.named_scope("gather_others"):
        others = jnp.concatenate([section_inputs, stashed_inputs[0, 1:]])
        gathered = halves(moved_rows(later(others, act_grad)))
    product = products(gathered[0], gain, up, [down])
    with jax.named_scope("swap_f0p"):
        parts = tensor_parts(product)
    ahead = [product]
    for turn in range(1, turn_count):
        stash_rows.append(gathered[turn])
        back_products.append(products(stash_rows[turn], gain, up, [down]))
        ahead.append(back_products[turn])
        with jax.named_scope("swap_b1p"):
            back_parts.append(tensor_parts(back_products[turn]))

    forward_results = []
    backward_results = []
    tables = []
    for turn in range(turn_count):
        with jax.named_scope(f"backward{turn}"):
            kept, sent, scaled, activated = backward(
                width, back_parts[turn], act_parts, stash_rows[turn], gain, up, down, ahead
            )
            back_pairs = scatter_pairs(kept, sent)
        tables.append((*stash_rows[turn], scaled, activated, *grad_halves))
        if turn + 1 == turn_count:
            with jax.named_scope(f"backward{turn}"):
                back_sums = scatter_parts(back_pairs)
            parts = later(parts, back_sums)
        with jax.named_scope(f"forward{turn}"):
            kept, sent = forward(width, parts, up, down, [])
            pairs = scatter_pairs(kept, sent)
        if turn + 1 == turn_count:
            with jax.named_scope(f"forward{turn}"):
                sums = scatter_parts(pairs)
            input_grads = finish(backward_results, grads_in, back_sums)
            section_outputs = finish(forward_results, rows_in, sums)
            break
        with jax.named_scope(f"scatter{turn}"):
            sums = scatter_parts(jnp.stack([back_pairs, pairs], axis=1))
        backward_results.append(added(grads_in, [part[0] for part in sums]))
        forward_results.append(added(rows_in, [part[1] for part in sums]))
        with jax.named_scope(f"gather{turn}"):
            moved = moved_passed(
                jnp.where(is_first, masked[turn], backward_results[-1]),
                jnp.where(is_last, entering[turn], forward_results[-1]),
            )
            passed = halves(later(moved, back_parts[turn + 1][1]))
        grad_halves = passed[0]
        grads_in, rows_in = passed[0][0][:local_rows], passed[1][0][:local_rows]
        act_grad = act_grads(grad_halves, up, down)
        with jax.named_scope("swap_b1a"):
            act_parts = tensor_parts(act_grad)
        product = products(later(passed[1], act_grad), gain, up, [down])
        with jax.named_scope("swap_f1p"):
            parts = tensor_parts(product)
        ahead = []
    return section_outputs, input_grads, tables


def body(
    section_inputs,
    entering,
    grad_outputs,
    arriving,
    live_rows,
    stashed_inputs,
    norm_gain,
    up_weight,
    down_weight,
    held_blocks,
    held_count,
    held_owner,
    first_moment,
    second_moment,
):
    section_count = lax.axis_size("section")
    section_index = lax.axis_index("section")
    dp_count = lax.axis_size("dp")
    turn_count = stashed_inputs.shape[1]
    local_rows = section_inputs.shape[1]
    channels, hidden = up_weight.shape[1:]
    width = channels * lax.axis_size("tensor")
    is_first = section_index == 0
    is_last = section_index == section_count - 1
    counts, owners, blocks = held_count[0, 0], held_owner[0, 0], held_blocks[0, 0]
    capacity = owners.shape[1]
    dp_index = lax.axis_index("dp")
    plan = jnp.concatenate([jnp.full((dp_count, 1), dp_index, jnp.int32), counts[:, None], owners, blocks], axis=1)

    def exchange(plan, tables, before):
        with jax.named_scope("block_exchange"):
            outgoing = outgoing_blocks(plan, capacity, norm_gain, tables, channels // BLK, hidden // BLK)
            outgoing = outgoing.reshape((2, dp_count // 2, BLK, BLK))
            relayed = later(sibling(outgoing[1]), before)
            pairs = [jnp.concatenate([outgoing[0, k], relayed[k]]) for k in range(1, dp_count // 2)]
            return relayed, [shifted(pair, -k - 1) for k, pair in enumerate(pairs)]

    if section_count == 2 and turn_count == 2:
        section_outputs, input_grads, plan, relayed, others, after = relay_pair(
            live_rows, arriving, entering, section_inputs[0], grad_outputs[0], stashed_inputs[0], norm_gain,
            up_weight[0], down_weight[0], width, plan, exchange,
        )
    else:
        row_ids = dp_index * local_rows + lax.iota(jnp.int32, local_rows)
        masked = jnp.where((row_ids < live_rows[:, None])[..., None], arriving, jnp.zeros((), BF16))
        section_outputs, input_grads, tables = relay(
            is_first, is_last, masked, entering, section_inputs, grad_outputs, stashed_inputs, norm_gain,
            up_weight[0], down_weight[0], width,
        )
        relayed, others = exchange(plan, tables, None)
        after = []
    first_out, second_out, direction_out = adam(
        plan, relayed, others, first_moment[0, 0, 0], second_moment[0, 0, 0], after
    )
    return (
        section_outputs[None],
        input_grads[None],
        first_out[None, None, None],
        second_out[None, None, None],
        direction_out[None, None, None],
    )


def solution(mesh):
    return jax.shard_map(
        body,
        mesh=mesh,
        in_specs=(
            P("section", "dp", "tensor"),
            P(None, "dp", "tensor"),
            P("section", "dp", "tensor"),
            P(None, "dp", "tensor"),
            P(),
            P("section", None, "dp", "tensor"),
            P("section", "tensor"),
            P("section", "tensor", "dp"),
            P("section", "dp", "tensor"),
            P("section", "tensor", None, None),
            P("section", "tensor", None),
            P("section", "tensor", None, None),
            P("section", "tensor", "dp", None, None, None),
            P("section", "tensor", "dp", None, None, None),
        ),
        out_specs=(
            P("section", None, "dp", "tensor"),
            P("section", None, "dp", "tensor"),
            P("section", "tensor", "dp", None, None, None),
            P("section", "tensor", "dp", None, None, None),
            P("section", "tensor", "dp", None, None, None),
        ),
        check_vma=False,
    )
```
